512 devices in a mesh: dp: 128 (over x, z, y_lo), tensor: 4 (over y_hi, core).
Axes of the slice: x: 4, y: 8 (y_hi: 2, y_lo: 4; y = y_hi * 4 + y_lo), z: 8, core: 2. Of those that a mesh axis runs over, the one named last changes fastest.
Arguments:
- images: bfloat16 [32768, 1152], P('dp'), may hold values from -6 to 6
- layer_norm_gain: float32 [1152], replicated, may hold values from 0.5 to 1.5
- hidden_weight: bfloat16 [1152, 4304], P('dp', 'tensor'), may hold values from -0.1875 to 0.1875
- output_weight: bfloat16 [4304, 1152], P('tensor', 'dp'), may hold values from -0.09375 to 0.09375
- text: bfloat16 [32768, 1152], P(('dp', 'tensor')), may hold values from -6 to 6
Outputs:
- images_gradient: float32 [32768, 1152], P('dp')
- grad_text: float32 [32768, 1152], P(('dp', 'tensor'))
The draws below stay inside these ranges and needn't reach their ends.
All inputs are finite; a program needn't handle non-finite values.
Results may differ from the reference program's by a relative error of at most 0.006.
Values may be sent and summed in bfloat16 or wider, within the bound.
A program may use at most 64 MiB of HBM per device.

```python
import jax
import jax.numpy as jnp
from jax import lax

D = 1152
FF = 4304
PAIRS_DEV = 256
HOPS = 8
BATCH = 32768
N_DP = 128


def levels(stream_key, shape, shards, low, largest):
    loudness, own = 1.0, jax.random.fold_in(stream_key, 6)
    for axis_at, blocks in shards:
        steps = jnp.exp(jax.random.uniform(jax.random.fold_in(own, axis_at), (blocks,), jnp.float32, low / len(shards), largest / len(shards)))
        loudness = loudness * jnp.repeat(steps, shape[axis_at] // blocks).reshape([-1 if axis == axis_at else 1 for axis in range(len(shape))])
    return loudness


def normal_values(key, extent, scale, reach, cuts=(), kind=jnp.bfloat16):
    result = jax.random.normal(key, extent, jnp.float32) * scale
    if len(cuts) > 0:
        result = levels(key, extent, cuts, -0.22, 0.18) * result
    return jnp.clip(result, min=-reach, max=reach).astype(kind)


def setup_inputs(seed: int = 0) -> dict:
    seeds = jax.random.split(jax.random.key(seed), 6)
    images = normal_values(seeds[0], (BATCH, D), 1.0, 6.0, ((0, 128),))
    layer_norm_gain = jnp.clip(1.0 + 0.1 * jax.random.normal(seeds[1], (D,), jnp.float32), 0.5, 1.5)
    hidden_weight = normal_values(seeds[2], (D, FF), D ** -0.5, 0.1875, ((0, 128), (1, 4)))
    output_weight = normal_values(seeds[3], (FF, D), FF ** -0.5, 0.09375, ((0, 4), (1, 128)))
    text = normal_values(seeds[4], (BATCH, D), 1.0, 6.0, ((0, 512),))
    return {"images": images, "layer_norm_gain": layer_norm_gain, "hidden_weight": hidden_weight, "output_weight": output_weight, "text": text}


SCALE_LOGIT = 10.0
BIAS_LOGIT = -3.0
EPS = 1e-06

def gelu_tanh(values):
    return jax.nn.gelu(values, approximate=True)

def unit_rows(values):
    row_norm = jnp.sqrt(lax.optimization_barrier(jnp.sum(values * values, axis=-1, keepdims=True)) + EPS)
    return (values / row_norm, row_norm)

def reference(images, layer_norm_gain, hidden_weight, output_weight, text):
    features = images.astype(jnp.float32)
    feature_mean = lax.optimization_barrier(jnp.mean(features, axis=1, keepdims=True))
    mean_shifted_input = features - feature_mean
    variance = lax.optimization_barrier(jnp.mean(mean_shifted_input * mean_shifted_input, axis=1, keepdims=True))
    reciprocal_deviation = 1.0 / jnp.sqrt(variance + EPS)
    standardized_input = mean_shifted_input * reciprocal_deviation
    normalized_input = (standardized_input * layer_norm_gain).astype(jnp.bfloat16)
    preact = jnp.dot(normalized_input, hidden_weight, preferred_element_type=jnp.float32)
    activated = gelu_tanh(preact).astype(jnp.bfloat16)
    head_out = features + jnp.dot(activated, output_weight, preferred_element_type=jnp.float32)
    image_f, image_norm = unit_rows(head_out)
    image_unit = image_f.astype(jnp.bfloat16)
    text_f, text_norm = unit_rows(text.astype(jnp.float32))
    text_unit = text_f.astype(jnp.bfloat16)
    half_hops = HOPS // 2
    offsets = jnp.arange(-half_hops, half_hops, dtype=jnp.int32)
    image_blocks = image_unit.reshape(N_DP, PAIRS_DEV, D)
    text_blocks = text_unit.reshape(N_DP, PAIRS_DEV, D)
    marker = jnp.concatenate([jnp.zeros((PAIRS_DEV, half_hops * PAIRS_DEV), jnp.float32), jnp.eye(PAIRS_DEV, dtype=jnp.float32), jnp.zeros((PAIRS_DEV, (half_hops - 1) * PAIRS_DEV), jnp.float32)], axis=1)

    def image_side(block_id):
        window = text_blocks[(block_id + offsets) % N_DP].reshape(HOPS * PAIRS_DEV, D)
        logits = SCALE_LOGIT * jnp.dot(image_blocks[block_id], window.T, preferred_element_type=jnp.float32) + BIAS_LOGIT
        slopes = (SCALE_LOGIT * (jax.nn.sigmoid(logits) - marker)).astype(jnp.bfloat16)
        return jnp.dot(slopes, window, preferred_element_type=jnp.float32)

    def text_side(block_id):
        window = image_blocks[(block_id - offsets) % N_DP].reshape(HOPS * PAIRS_DEV, D)
        logits = SCALE_LOGIT * jnp.dot(window, text_blocks[block_id].T, preferred_element_type=jnp.float32) + BIAS_LOGIT
        slopes = (SCALE_LOGIT * (jax.nn.sigmoid(logits) - marker.T)).astype(jnp.bfloat16)
        return jnp.dot(slopes.T, window, preferred_element_type=jnp.float32)
    block_ids = jnp.arange(N_DP, dtype=jnp.int32)
    grad_image_unit = lax.map(image_side, block_ids).reshape(N_DP * PAIRS_DEV, D)
    grad_text_unit = lax.map(text_side, block_ids).reshape(N_DP * PAIRS_DEV, D)
    grad_text = (grad_text_unit - text_f * lax.optimization_barrier(jnp.sum(text_f * grad_text_unit, axis=1, keepdims=True))) / text_norm
    output_gradient = (grad_image_unit - image_f * lax.optimization_barrier(jnp.sum(image_f * grad_image_unit, axis=1, keepdims=True))) / image_norm
    grad_out_b = output_gradient.astype(jnp.bfloat16)
    grad_act = jnp.dot(grad_out_b, output_weight.T, preferred_element_type=jnp.float32)
    pull_back = jax.vjp(gelu_tanh, preact)[1]
    grad_pre = pull_back(grad_act)[0].astype(jnp.bfloat16)
    normalized_gradient = jnp.dot(grad_pre, hidden_weight.T, preferred_element_type=jnp.float32)
    standardized_gradient = normalized_gradient * layer_norm_gain
    images_gradient = output_gradient + reciprocal_deviation * (standardized_gradient - lax.optimization_barrier(jnp.mean(standardized_gradient, axis=1, keepdims=True)) - standardized_input * lax.optimization_barrier(jnp.mean(standardized_gradient * standardized_input, axis=1, keepdims=True)))
    return (images_gradient, grad_text)
```

```python
import jax
import jax.numpy as jnp
import numpy as np
from jax import lax
from jax.experimental import pallas as pl
from jax.experimental.pallas import tpu as pltpu
from jax.sharding import PartitionSpec as P

SCALE_LOGIT = 10.0
BIAS_LOGIT = -3.0
EPS = 1e-06

NX, NZ, NY, NLO = 4, 8, 8, 4
D = 1152
FW = 1152
OWN = 9
MESH = pl.DeviceIdType.MESH
BF = jnp.bfloat16
F32 = jnp.float32
GELU_C = 0.7978845608028654
GELU_A = 0.044715


def contract_last(left, right):
    return lax.dot_general(left, right, (((1,), (1,)), ((), ())), preferred_element_type=F32)


def ident(x, z, y, c):
    return (x * (NZ * NLO) + z * NLO + lax.rem(y, NLO), (y // NLO) * 2 + c)


class Ring:
    def __init__(self, buf, size, pos, after, before, chunks, half, ssem, rsem):
        self.buf, self.size, self.pos = buf, size, pos
        self.rows = buf.shape[0] // size
        self.peer = (after, before)
        self.chunks, self.half = chunks, half
        self.ssem, self.rsem = ssem, rsem
        self.steps = size // 2

    def own(self):
        return pl.ds(pl.multiple_of(self.pos * self.rows, 16), self.rows)

    def kept(self, step, way):
        ids = list(range(len(self.chunks)))
        if step < self.steps:
            return ids
        return ids[: self.half] if way == 0 else ids[self.half :]

    def copy(self, step, way, ch, back):
        move = back if way == 0 else -back
        slot = lax.rem(self.pos - move + 2 * self.size, self.size)
        off, rows = self.chunks[ch]
        ref = self.buf.at[pl.ds(pl.multiple_of(slot * self.rows + off, 16), rows)]
        return pltpu.make_async_remote_copy(
            src_ref=ref,
            dst_ref=ref,
            send_sem=self.ssem.at[step - 1, way, ch],
            recv_sem=self.rsem.at[step - 1, way, ch],
            device_id=self.peer[way],
            device_id_type=MESH,
        )

    def each(self, step):
        for ch in range(len(self.chunks)):
            for way in (0, 1):
                if ch in self.kept(step, way):
                    yield way, ch

    def start(self):
        for way, ch in self.each(1):
            self.copy(1, way, ch, 0).start()

    def forward(self, step):
        for way, ch in self.each(step):
            self.copy(step, way, ch, step).wait_recv()
            if step < self.steps and ch in self.kept(step + 1, way):
                self.copy(step + 1, way, ch, step).start()

    def finish(self):
        for step in range(1, self.steps + 1):
            for way, ch in self.each(step):
                self.copy(step, way, ch, step - 1).wait_send()


CH48 = ((0, 32), (32, 16))
CH144 = ((0, 48), (48, 32), (80, 32), (112, 32))
CH288 = ((0, 80), (80, 64), (144, 80), (224, 64))


def pack_matrix(groups, rows_in, rows_out, used):
    shape = (rows_out, groups * rows_in)
    row = lax.broadcasted_iota(jnp.int32, shape, 0)
    col = lax.broadcasted_iota(jnp.int32, shape, 1)
    hit = jnp.zeros(shape, F32)
    for g in range(groups):
        inner = col - g * rows_in
        hit = jnp.where((inner >= 0) & (inner < used) & (row == inner + g * used), 1.0, hit)
    return hit.astype(BF)


def column_loop(body):
    @pl.loop(0, 3)
    def _(k):
        body(pl.ds(pl.multiple_of(k * 384, 128), 384))


def ln_stats(v):
    v = v - jnp.sum(v, axis=1, keepdims=True) * (1.0 / D)
    var = jnp.sum(v * v, axis=1, keepdims=True) * (1.0 / D)
    rdev = 1.0 / jnp.sqrt(var + EPS)
    return v * rdev, rdev


def kernel(
    images, gain, h_own, o_own, text, order,
    out_img, out_text,
    hy, oy, hx, hz, oz, ox, xin, perm, npm, act, preact, dgel, part,
    cs, cr, es, er, unit, head, inorm, gout, gob, gpre, texts, tunit, tgs, tgr, slopes, slopes_t, accb, gnat,
    y_ss, y_rs, im_ss, im_rs, hx_ss, hx_rs, hz_ss, hz_rs, oz_ss, oz_rs, ox_ss, ox_rs,
    tx_ss, tx_rs, tg_ss, tg_rs, sw_ss, sw_rs,
):
    a = lax.axis_index("dp")
    t = lax.axis_index("tensor")
    x, z, lo = a // (NZ * NLO), lax.rem(a // NLO, NZ), lax.rem(a, NLO)
    h, c = t // 2, lax.rem(t, 2)
    y = h * NLO + lo
    p = lax.rem(lo, 2)
    q = p * 2 + c
    a0 = a - p
    n_dp = NX * NZ * NLO
    mine = p == h

    core = ident(x, z, y, 1 - c)
    pair = ident(x, z, y + 1 - 2 * p, c)
    far = ident(x, z, lax.rem(y + NLO, NY), c)
    x_up = ident(lax.rem(x + 1, NX), z, y, c)
    x_dn = ident(lax.rem(x + NX - 1, NX), z, y, c)
    z_up = ident(x, lax.rem(z + 1, NZ), y, c)
    z_dn = ident(x, lax.rem(z + NZ - 1, NZ), y, c)

    def owner(j):
        return (lax.rem(a0 - 4 + j + n_dp, n_dp), q)

    def user(i, half):
        return (lax.rem(a - p - 4 + 2 * i + h + n_dp, n_dp), half * 2 + c)

    def each_owner(body):
        for j in range(9):

            @pl.when(jnp.logical_not(mine & (p + 4 == j)))
            def _():
                body(j)

    def each_user(body):
        for i in range(5):
            for half in range(2):
                here = jnp.logical_not(mine & (h == half)) if i == 2 else None
                if i == 0:
                    here = p == 0
                if here is None:
                    body(i, half)
                else:

                    @pl.when(here)
                    def _():
                        body(i, half)

    def remote(src, dst, ss, rs, device):
        return pltpu.make_async_remote_copy(
            src_ref=src, dst_ref=dst, send_sem=ss, recv_sem=rs, device_id=device, device_id_type=MESH
        )

    def slab(k, rows):
        return pl.ds(k * rows if isinstance(k, int) else pl.multiple_of(k * rows, rows), rows)

    bar = pltpu.get_barrier_semaphore()

    def signal(device):
        pl.semaphore_signal(bar, inc=1, device_id=device, device_id_type=MESH)

    for device in (core, pair, far, x_up, x_dn, z_up, z_dn):
        signal(device)
    for l in range(NLO):

        @pl.when(jnp.logical_not((4 * p + l) == y))
        def _():
            signal(ident(x, z, 4 * p + l, c))

    each_owner(lambda j: signal(owner(j)))
    each_user(lambda i, half: signal(user(i, half)))
    pl.semaphore_wait(bar, 30 - 3 * mine.astype(jnp.int32) - 2 * p)

    for which, (src, dst) in enumerate(((h_own, hy), (o_own, oy))):
        for i in range(4):

            @pl.when(jnp.logical_not((h + 2 * i) == y))
            def _():
                remote(
                    src, dst.at[slab(lo, 16)], y_ss.at[which, i], y_rs.at[which, lo], ident(x, z, h + 2 * i, c)
                ).start()

            @pl.when((h + 2 * i) == y)
            def _():
                dst[slab(lo, 16), :] = src[...]

    def im_copy(k, block):
        return remote(
            images.at[slab(2 * h + k, 64)], xin.at[slab(2 * k + block, 64)], im_ss.at[k], im_rs.at[k], pair
        )

    for k in range(2):
        im_copy(k, p).start()
        xin[slab(2 * k + p, 64), :] = images[slab(2 * h + k, 64), :]

    tx = text[...].astype(F32)
    text_norm = jnp.sqrt(jnp.sum(tx * tx, axis=1, keepdims=True) + EPS)
    tunit[...] = (tx / text_norm).astype(BF)

    def tx_copy(i, half):
        j = p + 8 - 2 * i
        return remote(tunit, texts.at[slab(j, 64)], tx_ss.at[i, half], tx_rs.at[j], user(i, half))

    each_user(lambda i, half: tx_copy(i, half).start())
    texts[slab(9, 64), :] = jnp.zeros((64, D), BF)

    @pl.when(mine)
    def _():
        texts[slab(p + 4, 64), :] = tunit[...]

    @pl.when(p == 1)
    def _():
        tgr[pl.ds(0, 128), :] = jnp.zeros((128, D), BF)

    ring_hx = Ring(hx, NX, x, x_up, x_dn, CH48, 1, hx_ss, hx_rs)
    ring_hz = Ring(hz, NZ, z, z_up, z_dn, CH144, 2, hz_ss, hz_rs)
    ring_oz = Ring(oz, NZ, z, z_up, z_dn, CH48, 1, oz_ss, oz_rs)
    ring_ox = Ring(ox, NX, x, x_up, x_dn, CH288, 2, ox_ss, ox_rs)

    pack_y = pack_matrix(NLO, 16, 48, OWN)

    def y_wait(which, src, dst):
        for l in range(NLO):

            @pl.when(jnp.logical_not((4 * p + l) == y))
            def _():
                remote(src, dst.at[slab(l, 16)], y_ss.at[which, 0], y_rs.at[which, l], pair).wait_recv()

    y_wait(0, h_own, hy)
    hx[ring_hx.own(), :] = jnp.dot(pack_y, hy[...], preferred_element_type=F32).astype(BF)
    ring_hx.start()
    y_wait(1, o_own, oy)
    oz[ring_oz.own(), :] = jnp.dot(pack_y, oy[...], preferred_element_type=F32).astype(BF)
    ring_oz.start()
    ring_hx.forward(1)
    ring_oz.forward(1)
    ring_hx.forward(2)
    pack_x = pack_matrix(NX, 48, 144, 4 * OWN)
    hz[ring_hz.own(), :] = jnp.dot(pack_x, hx[...], preferred_element_type=F32).astype(BF)
    ring_oz.forward(2)
    ring_hz.start()
    ring_oz.forward(3)

    @pl.loop(0, 9)
    def _(k):
        rows = lax.broadcasted_iota(jnp.int32, (128, D), 0) + k * 128
        perm[slab(k, 128), :] = jnp.where(rows == order[...], 1.0, 0.0).astype(BF)

    for k in range(2):
        im_copy(k, 1 - p).wait_recv()

    @pl.loop(0, 4)
    def _(r):
        xhat, _ = ln_stats(xin[slab(r, 64), :].astype(F32))
        unit[slab(r, 64), :] = (xhat * gain[...]).astype(BF)

    def permute_normed(cols):
        npm[:, cols] = jnp.dot(unit[...], perm[:, cols], preferred_element_type=F32).astype(BF)

    column_loop(permute_normed)

    ring_oz.forward(4)

    def pack_ox(cols):
        pack_z = pack_matrix(NZ, 48, 288, 4 * OWN)
        ox[ring_ox.own(), cols] = jnp.dot(pack_z, oz[:, cols], preferred_element_type=F32).astype(BF)

    column_loop(pack_ox)
    ring_ox.start()
    ring_hz.forward(1)
    ring_hz.forward(2)
    ring_ox.forward(1)
    ring_hz.forward(3)
    ring_hz.forward(4)

    def hidden(cols):
        v = jnp.dot(npm[...], hz[:, cols], preferred_element_type=F32)
        preact[:, cols] = v
        act[:, cols] = (0.5 * v * (1.0 + jnp.tanh(GELU_C * (v + GELU_A * (v * v * v))))).astype(BF)

    column_loop(hidden)
    ring_ox.forward(2)

    def head_terms(cols):
        part[:, cols] = contract_last(act[...], ox[cols, :])

    column_loop(head_terms)

    own_rows = slab(c, 128)
    other_rows = slab(1 - c, 128)

    def swap(n, src, dst, device):
        return remote(src, dst, sw_ss.at[n], sw_rs.at[n], device)

    def core_sum(n, k):
        cs[slab(k, 128), :] = part[other_rows, :].astype(BF)
        move = swap(n, cs.at[slab(k, 128)], cr.at[slab(k, 128)], core)
        move.start()
        move.wait_recv()
        accb[...] = part[own_rows, :] + cr[slab(k, 128), :].astype(F32)
        return move

    moves = [core_sum(0, 0)]
    es[slab(0, 128), :] = accb[...].astype(BF)
    moves.append(swap(1, es.at[slab(0, 128)], er.at[slab(0, 128)], pair))
    moves[-1].start()

    def gelu_slope(cols):
        v = preact[:, cols]
        th = jnp.tanh(GELU_C * (v + GELU_A * (v * v * v)))
        inner = GELU_C * (1.0 + (3.0 * GELU_A) * (v * v))
        dgel[:, cols] = 0.5 * (1.0 + th) + 0.5 * v * (1.0 - th * th) * inner

    column_loop(gelu_slope)
    moves[-1].wait_recv()

    @pl.loop(0, 2)
    def _(b):
        rows = slab(b, 64)
        out = xin[slab(2 * c + b, 64), :].astype(F32) + accb[rows, :] + er[rows, :].astype(F32)
        norm = jnp.sqrt(jnp.sum(out * out, axis=1, keepdims=True) + EPS)
        out = out / norm
        head[rows, :] = out
        inorm[rows, :] = jnp.broadcast_to(norm, (64, 128))
        unit[slab(2 * c + b, 64), :] = out.astype(BF)

    moves.append(swap(2, unit.at[own_rows], unit.at[own_rows], core))
    moves[-1].start()
    each_owner(lambda j: remote(tunit, texts.at[slab(j, 64)], tx_ss.at[0, 0], tx_rs.at[j], pair).wait_recv())
    swap(2, unit.at[other_rows], unit.at[other_rows], core).wait_recv()

    own_quarter = 2 * h

    def slope(dots, row, col):
        block = lax.shift_right_logical(row, 6) & 1
        scored = (col >= block * 64) & (col < 512 + block * 64)
        match = (col == 256 + block * 64 + (row & 63)) & (lax.shift_right_logical(row, 7) + own_quarter == q)
        value = jax.nn.sigmoid(SCALE_LOGIT * dots + BIAS_LOGIT) - jnp.where(match, 1.0, 0.0)
        return jnp.where(scored, SCALE_LOGIT * value, 0.0).astype(BF)

    @pl.loop(0, 5)
    def _(k):
        cols = slab(k, 128)
        row = lax.broadcasted_iota(jnp.int32, (256, 128), 0)
        col = lax.broadcasted_iota(jnp.int32, (256, 128), 1) + k * 128
        slopes[:, cols] = slope(contract_last(unit[...], texts[cols, :]), row, col)

    def to_image(cols):
        part[:, cols] = jnp.dot(slopes[...], texts[:, cols], preferred_element_type=F32)

    column_loop(to_image)
    moves.append(core_sum(3, 1))
    es[slab(1, 128), :] = accb[...].astype(BF)
    moves.append(swap(4, es.at[slab(1, 128)], er.at[slab(1, 128)], pair))
    moves[-1].start()

    @pl.loop(0, 5)
    def _(k):
        rows = slab(k, 128)
        row = lax.broadcasted_iota(jnp.int32, (128, 256), 1)
        col = lax.broadcasted_iota(jnp.int32, (128, 256), 0) + k * 128
        slopes_t[rows, :] = slope(contract_last(texts[rows, :], unit[...]), row, col)

    def to_text(cols):
        tgs[:, cols] = jnp.dot(slopes_t[...], unit[:, cols], preferred_element_type=F32).astype(BF)

    column_loop(to_text)

    moves[-1].wait_recv()

    @pl.loop(0, 2)
    def _(b):
        rows = slab(b, 64)
        g = accb[rows, :] + er[pl.ds(pl.multiple_of(128 + b * 64, 64), 64), :].astype(F32)
        f = head[rows, :]
        out = (g - f * jnp.sum(f * g, axis=1, keepdims=True)) / inorm[rows, 0:1]
        gout[rows, :] = out
        gob[slab(2 * c + b, 64), :] = out.astype(BF)

    moves.append(swap(5, gob.at[own_rows], gob.at[own_rows], core))
    moves[-1].start()

    def tg_copy(j):
        i = (j % 2 + 8 - j) // 2
        return remote(
            tgs.at[slab(j, 64)], tgr.at[slab(2 * i + h, 64)], tg_ss.at[j], tg_rs.at[2 * i + h], owner(j)
        )

    each_owner(lambda j: tg_copy(j).start())

    @pl.when(mine)
    def _():
        tgr[slab(4 + h, 64), :] = tgs[slab(4 + p, 64), :]

    swap(5, gob.at[other_rows], gob.at[other_rows], core).wait_recv()

    def hidden_back(cols):
        g = jnp.dot(gob[...], ox[:, cols], preferred_element_type=F32)
        gpre[:, cols] = (g * dgel[:, cols]).astype(BF)

    column_loop(hidden_back)

    def normed_terms(cols):
        part[:, cols] = contract_last(gpre[...], hz[cols, :])

    column_loop(normed_terms)
    moves.append(core_sum(6, 2))
    es[pl.ds(256, 64), :] = accb[slab(1 - p, 64), :].astype(BF)
    moves.append(swap(7, es.at[pl.ds(256, 64)], er.at[pl.ds(256, 64)], pair))
    moves[-1].start()
    xhat, rdev = ln_stats(xin[slab(2 * c + p, 64), :].astype(F32))
    moves[-1].wait_recv()
    total = accb[slab(p, 64), :] + er[pl.ds(256, 64), :].astype(F32)
    high = total.astype(BF)
    low = (total - high.astype(F32)).astype(BF)

    @pl.loop(0, 3)
    def _(k):
        cols = pl.ds(pl.multiple_of(k * 384, 128), 384)
        gnat[:, cols] = contract_last(high, perm[cols, :]) + contract_last(low, perm[cols, :])

    g = gnat[...] * gain[...]
    mean_g = jnp.sum(g, axis=1, keepdims=True) * (1.0 / D)
    mean_gx = jnp.sum(g * xhat, axis=1, keepdims=True) * (1.0 / D)
    done = slab(2 * h + c, 64)
    out_img[done, :] = (gout[slab(p, 64), :] + rdev * (g - mean_g - xhat * mean_gx)).astype(BF)
    for n, device in ((8, far), (9, core)):
        moves.append(swap(n, out_img.at[done], out_img.at[done], device))
        moves[-1].start()

    each_user(lambda i, half: remote(
        tunit, tgr.at[slab(2 * i + half, 64)], tg_ss.at[0], tg_rs.at[2 * i + half], pair
    ).wait_recv())
    g = tgr[pl.ds(0, 64), :].astype(F32)
    for k in range(1, 10):
        g = g + tgr[slab(k, 64), :].astype(F32)
    tx = text[...].astype(F32)
    text_norm = jnp.sqrt(jnp.sum(tx * tx, axis=1, keepdims=True) + EPS)
    text_f = tx / text_norm
    out_text[...] = (g - text_f * jnp.sum(text_f * g, axis=1, keepdims=True)) / text_norm

    from_far = slab(2 * (1 - h) + c, 64)
    swap(8, out_img.at[from_far], out_img.at[from_far], far).wait_recv()
    moves.append(swap(10, out_img.at[from_far], out_img.at[from_far], core))
    moves[-1].start()
    from_core = slab(2 * h + 1 - c, 64)
    swap(9, out_img.at[from_core], out_img.at[from_core], core).wait_recv()
    from_both = slab(2 * (1 - h) + 1 - c, 64)
    swap(10, out_img.at[from_both], out_img.at[from_both], core).wait_recv()

    for which, (src, dst) in enumerate(((h_own, hy), (o_own, oy))):
        for i in range(4):

            @pl.when(jnp.logical_not((h + 2 * i) == y))
            def _():
                remote(
                    src, dst.at[slab(lo, 16)], y_ss.at[which, i], y_rs.at[which, lo], ident(x, z, h + 2 * i, c)
                ).wait_send()

    for k in range(2):
        im_copy(k, p).wait_send()
    each_user(lambda i, half: tx_copy(i, half).wait_send())
    each_owner(lambda j: tg_copy(j).wait_send())
    for ring in (ring_hx, ring_hz, ring_oz, ring_ox):
        ring.finish()
    for move in moves:
        move.wait_send()


def feature_order():
    z, x, j = np.meshgrid(np.arange(NZ), np.arange(NX), np.arange(NLO * OWN), indexing="ij")
    return (x * (NZ * NLO * OWN) + z * (NLO * OWN) + j).reshape(1, D).astype(np.int32)


def shards(images, layer_norm_gain, hidden_weight, output_weight, text):
    width = hidden_weight.shape[1]
    pad = ((0, 16 - OWN), (0, FW - width))
    h_own = jnp.pad(hidden_weight, pad)
    o_own = jnp.pad(output_weight.T, pad)

    def vm(rows, cols, kind=BF):
        return pltpu.VMEM((rows, cols), kind)

    dma = pltpu.SemaphoreType.DMA
    scratch = [
        vm(64, FW), vm(64, FW), vm(192, FW), vm(D, FW), vm(384, FW), vm(D, FW),
        vm(256, D), vm(D, D), vm(256, D), vm(256, FW), vm(256, FW, F32), vm(256, FW, F32), vm(256, D, F32),
        vm(384, D), vm(384, D), vm(320, D), vm(320, D),
        vm(256, D), vm(128, D, F32), vm(128, 128, F32), vm(128, D, F32), vm(256, D), vm(256, FW),
        vm(640, D), vm(64, D), vm(640, D), vm(640, D), vm(256, 640), vm(640, 256), vm(128, D, F32), vm(64, D, F32),
        dma((2, 4)), dma((2, 4)), dma((2,)), dma((2,)),
        dma((2, 2, 2)), dma((2, 2, 2)), dma((4, 2, 4)), dma((4, 2, 4)),
        dma((4, 2, 2)), dma((4, 2, 2)), dma((2, 2, 4)), dma((2, 2, 4)),
        dma((5, 2)), dma((9,)), dma((9,)), dma((10,)), dma((11,)), dma((11,)),
    ]
    vmem = pl.BlockSpec(memory_space=pltpu.VMEM)
    images_gradient, grad_text = pl.pallas_call(
        kernel,
        out_shape=(jax.ShapeDtypeStruct((256, D), BF), jax.ShapeDtypeStruct((64, D), F32)),
        in_specs=[vmem] * 6,
        out_specs=(vmem, vmem),
        scratch_shapes=scratch,
        compiler_params=pltpu.CompilerParams(
            collective_id=0, has_side_effects=True, vmem_limit_bytes=56 * 2**20
        ),
        cost_estimate=pl.CostEstimate(flops=4 * 10**9, bytes_accessed=4 * 10**6, transcendentals=10**6),
    )(images, layer_norm_gain.reshape(1, D), h_own, o_own, text, jnp.asarray(feature_order()))
    return images_gradient.astype(F32), grad_text


def solution(mesh):
    placed = (P("dp", None), P(), P("dp", "tensor"), P("tensor", "dp"), P(("dp", "tensor"), None))
    return jax.shard_map(
        shards,
        mesh=mesh,
        in_specs=placed,
        out_specs=(P("dp", None), P(("dp", "tensor"), None)),
        check_vma=False,
    )
```

```python
import jax
import jax.numpy as jnp
import numpy as np
from jax import lax
from jax.experimental import pallas as pl
from jax.experimental.pallas import tpu as pltpu
from jax.sharding import PartitionSpec as P

SCALE_LOGIT = 10.0
BIAS_LOGIT = -3.0
EPS = 1e-06

NX, NZ, NY, NLO = 4, 8, 8, 4
D = 1152
FW = 1152
OWN = 9
MESH = pl.DeviceIdType.MESH
BF = jnp.bfloat16
F32 = jnp.float32
GELU_C = 0.7978845608028654
GELU_A = 0.044715


def contract_last(left, right):
    return lax.dot_general(left, right, (((1,), (1,)), ((), ())), preferred_element_type=F32)


def ident(x, z, y, c):
    return (x * (NZ * NLO) + z * NLO + lax.rem(y, NLO), (y // NLO) * 2 + c)


class Net:
    def __init__(self):
        self.sends, self.arrivals = [], {}

    def start(self, copy, name, arrival=None):
        copy.start()
        self.sends.append(copy.wait_send)
        self.arrivals[name] = (arrival or copy).wait_recv

    def wait(self, name):
        self.arrivals.pop(name)()

    def drain(self):
        for name in list(self.arrivals):
            self.wait(name)
        for wait_send in self.sends:
            wait_send()


class Ring:
    def __init__(self, net, buf, size, pos, after, before, chunks, half, ssem, rsem):
        self.net, self.buf, self.size, self.pos = net, buf, size, pos
        self.rows = buf.shape[0] // size
        self.peer = (after, before)
        self.chunks, self.half = chunks, half
        self.ssem, self.rsem = ssem, rsem
        self.steps = size // 2

    def own(self):
        return pl.ds(pl.multiple_of(self.pos * self.rows, 16), self.rows)

    def kept(self, step, way):
        ids = list(range(len(self.chunks)))
        if step < self.steps:
            return ids
        return ids[: self.half] if way == 0 else ids[self.half :]

    def copy(self, step, way, ch, back):
        move = back if way == 0 else -back
        slot = lax.rem(self.pos - move + 2 * self.size, self.size)
        off, rows = self.chunks[ch]
        ref = self.buf.at[pl.ds(pl.multiple_of(slot * self.rows + off, 16), rows)]
        return pltpu.make_async_remote_copy(
            src_ref=ref,
            dst_ref=ref,
            send_sem=self.ssem.at[step - 1, way, ch],
            recv_sem=self.rsem.at[step - 1, way, ch],
            device_id=self.peer[way],
            device_id_type=MESH,
        )

    def each(self, step):
        for ch in range(len(self.chunks)):
            for way in (0, 1):
                if ch in self.kept(step, way):
                    yield way, ch

    def send(self, step, way, ch):
        sent, comes = self.copy(step, way, ch, step - 1), self.copy(step, way, ch, step)
        self.net.start(sent, (self, step, way, ch), comes)

    def start(self):
        for way, ch in self.each(1):
            self.send(1, way, ch)

    def forward(self, step):
        for way, ch in self.each(step):
            self.net.wait((self, step, way, ch))
            if step < self.steps and ch in self.kept(step + 1, way):
                self.send(step + 1, way, ch)


CH48 = ((0, 32), (32, 16))
CH144 = ((0, 48), (48, 32), (80, 32), (112, 32))
CH288 = ((0, 80), (80, 64), (144, 80), (224, 64))


def pack_matrix(groups, rows_in, rows_out, used):
    shape = (rows_out, groups * rows_in)
    row = lax.broadcasted_iota(jnp.int32, shape, 0)
    col = lax.broadcasted_iota(jnp.int32, shape, 1)
    hit = jnp.zeros(shape, F32)
    for g in range(groups):
        inner = col - g * rows_in
        hit = jnp.where((inner >= 0) & (inner < used) & (row == inner + g * used), 1.0, hit)
    return hit.astype(BF)


def column_loop(body):
    @pl.loop(0, 3)
    def _(k):
        body(pl.ds(pl.multiple_of(k * 384, 128), 384))


def ln_stats(v):
    v = v - jnp.sum(v, axis=1, keepdims=True) * (1.0 / D)
    var = jnp.sum(v * v, axis=1, keepdims=True) * (1.0 / D)
    rdev = 1.0 / jnp.sqrt(var + EPS)
    return v * rdev, rdev


def stages(
    net, images, gain_in, h_in, o_in, text, order,
    out_img, out_text,
    h_own, o_own, hy, oy, hx, hz, oz, ox, xin, perm, npm, act, preact, dgel, part,
    cs, cr, es, er, unit, head, inorm, gout, gob, gpre, texts, tz, tgs, from_next, from_last, tgy, tgr, slopes, slopes_t, accb, gnat,
    y_ss, y_rs, im_ss, im_rs, hx_ss, hx_rs, hz_ss, hz_rs, oz_ss, oz_rs, ox_ss, ox_rs,
    tz_ss, tz_rs, tx_ss, tx_rs, gz_ss, gz_rs, tg_ss, tg_rs, sw_ss, sw_rs,
):
    a = lax.axis_index("dp")
    t = lax.axis_index("tensor")
    x, z, lo = a // (NZ * NLO), lax.rem(a // NLO, NZ), lax.rem(a, NLO)
    h, c = t // 2, lax.rem(t, 2)
    y = h * NLO + lo
    p = lax.rem(lo, 2)
    q = p * 2 + c
    kk = lo // 2
    n_dp = NX * NZ * NLO
    mine = p == h

    core = ident(x, z, y, 1 - c)
    pair = ident(x, z, y + 1 - 2 * p, c)
    far = ident(x, z, lax.rem(y + NLO, NY), c)
    x_up = ident(lax.rem(x + 1, NX), z, y, c)
    x_dn = ident(lax.rem(x + NX - 1, NX), z, y, c)
    z_up = ident(x, lax.rem(z + 1, NZ), y, c)
    z_dn = ident(x, lax.rem(z + NZ - 1, NZ), y, c)

    last = (lax.rem(a - NLO + n_dp, n_dp), t)
    after = (lax.rem(a + NLO, n_dp), t)

    def ring_y(k):
        return ident(x, z, k, c)

    def when(*conditions):
        live = [k for k in conditions if not isinstance(k, bool)]
        if not all(k for k in conditions if isinstance(k, bool)):
            return lambda body: None
        if not live:
            return lambda body: body()
        both = live[0]
        for k in live[1:]:
            both = both & k
        return pl.when(both)

    takers = [h + 2 * i for i in range(4)]
    holders = [4 * p + l for l in range(NLO)]

    def other(k):
        return jnp.logical_not(k == y)

    def remote(src, dst, ss, rs, device):
        return pltpu.make_async_remote_copy(
            src_ref=src, dst_ref=dst, send_sem=ss, recv_sem=rs, device_id=device, device_id_type=MESH
        )

    def slab(k, rows):
        return pl.ds(k * rows if isinstance(k, int) else pl.multiple_of(k * rows, rows), rows)

    from_next[...] = jnp.zeros((256, D), BF)
    from_last[...] = jnp.zeros((256, D), BF)
    gain = gain_in[...].reshape(1, D)
    h_own[...] = jnp.zeros((16, FW), BF)
    h_own[pl.ds(0, OWN), pl.ds(0, h_in.shape[1])] = h_in[...]
    o_own[...] = jnp.zeros((16, FW), BF)
    turn = lax.broadcasted_iota(jnp.int32, (16, OWN), 0) == lax.broadcasted_iota(jnp.int32, (16, OWN), 1)
    o_own[:, pl.ds(0, o_in.shape[0])] = contract_last(jnp.where(turn, 1.0, 0.0).astype(BF), o_in[...]).astype(BF)

    bar = pltpu.get_barrier_semaphore()

    def signal(device):
        pl.semaphore_signal(bar, inc=1, device_id=device, device_id_type=MESH)

    for device in (core, pair, far, x_up, x_dn, z_up, z_dn, last, after):
        signal(device)
    for k in takers + holders:

        @pl.when(other(k))
        def _():
            signal(ring_y(k))

    pl.semaphore_wait(bar, 17 - 2 * mine.astype(jnp.int32))

    def y_copy(which, src, dst, i):
        to = ident(x, z, h + 2 * i, c)
        return remote(src, dst.at[slab(lo, 16)], y_ss.at[which, i], y_rs.at[which, lo], to)

    def y_sent(which, src, dst):
        for i in range(4):

            @pl.when(jnp.logical_not((h + 2 * i) == y))
            def _():
                y_copy(which, src, dst, i).wait_send()

    def y_wait(which, src, dst):
        for l in range(NLO):

            @pl.when(jnp.logical_not((4 * p + l) == y))
            def _():
                remote(src, dst.at[slab(l, 16)], y_ss.at[which, 0], y_rs.at[which, l], pair).wait_recv()

    for which, (src, dst) in enumerate(((h_own, hy), (o_own, oy))):
        for i in range(4):

            @pl.when(jnp.logical_not((h + 2 * i) == y))
            def _():
                y_copy(which, src, dst, i).start()

            @pl.when((h + 2 * i) == y)
            def _():
                dst[slab(lo, 16), :] = src[...]

        net.sends.append(lambda which=which, src=src, dst=dst: y_sent(which, src, dst))
        net.arrivals["y", which] = lambda which=which, src=src, dst=dst: y_wait(which, src, dst)

    def im_copy(k, block):
        return remote(
            images.at[slab(2 * h + k, 64)], xin.at[slab(2 * k + block, 64)], im_ss.at[k], im_rs.at[k], pair
        )

    for k in range(2):
        net.start(im_copy(k, p), ("im", k), im_copy(k, 1 - p))
        xin[slab(2 * k + p, 64), :] = images[slab(2 * h + k, 64), :]

    tx = text[...].astype(F32)
    text_norm = jnp.sqrt(jnp.sum(tx * tx, axis=1, keepdims=True) + EPS)
    tz[pl.ds(64, 64), :] = (tx / text_norm).astype(BF)
    for d, (device, back) in enumerate(((after, last), (last, after))):
        mine_tz, there, here = tz.at[pl.ds(64, 64)], tz.at[pl.ds(128 * d, 64)], tz.at[pl.ds(128 * d, 64)]
        net.start(
            remote(mine_tz, there, tz_ss.at[d], tz_rs.at[d], device), ("tz", d),
            remote(mine_tz, here, tz_ss.at[d], tz_rs.at[d], back),
        )

    def text_slot(i, d):
        k = i % 2
        used = {(0, 2): lo == 0, (1, 0): lo >= 2, (1, 2): lo <= 2}.get((k, d), True)
        return 4 * d + lo - 2 * k, used

    def tx_copy(i, d):
        j, _ = text_slot(i, d)
        return remote(
            tz.at[pl.ds(64 * d, 64)], texts.at[slab(j, 64)], tx_ss.at[i, d], tx_rs.at[j], ring_y(takers[i])
        )

    def tx_send(d):
        for i in range(4):
            j, used = text_slot(i, d)

            @when(used, other(takers[i]))
            def _():
                tx_copy(i, d).start()

            @when(used, takers[i] == y)
            def _():
                texts[slab(j, 64), :] = tz[pl.ds(64 * d, 64), :]

    def tx_sent():
        for d in range(3):
            for i in range(4):

                @when(text_slot(i, d)[1], other(takers[i]))
                def _():
                    tx_copy(i, d).wait_send()

    def tx_wait():
        for j in range(9):

            @when(jnp.logical_not(mine & (p == j % 4)))
            def _():
                remote(
                    tz.at[pl.ds(64, 64)], texts.at[slab(j, 64)], tx_ss.at[0, 0], tx_rs.at[j], pair
                ).wait_recv()

    tx_send(1)
    net.sends.append(tx_sent)
    net.arrivals["tx"] = tx_wait
    texts[slab(9, 64), :] = jnp.zeros((64, D), BF)

    ring_hx = Ring(net, hx, NX, x, x_up, x_dn, CH48, 1, hx_ss, hx_rs)
    ring_hz = Ring(net, hz, NZ, z, z_up, z_dn, CH144, 2, hz_ss, hz_rs)
    ring_oz = Ring(net, oz, NZ, z, z_up, z_dn, CH48, 1, oz_ss, oz_rs)
    ring_ox = Ring(net, ox, NX, x, x_up, x_dn, CH288, 2, ox_ss, ox_rs)

    pack_y = pack_matrix(NLO, 16, 48, OWN)

    net.wait(("y", 0))
    hx[ring_hx.own(), :] = jnp.dot(pack_y, hy[...], preferred_element_type=F32).astype(BF)
    ring_hx.start()
    for d in (0, 1):
        net.wait(("tz", d))
        tx_send(2 * d)
    net.wait(("y", 1))
    oz[ring_oz.own(), :] = jnp.dot(pack_y, oy[...], preferred_element_type=F32).astype(BF)
    ring_oz.start()
    ring_hx.forward(1)
    ring_oz.forward(1)
    ring_hx.forward(2)
    pack_x = pack_matrix(NX, 48, 144, 4 * OWN)
    hz[ring_hz.own(), :] = jnp.dot(pack_x, hx[...], preferred_element_type=F32).astype(BF)
    ring_oz.forward(2)
    ring_hz.start()
    ring_oz.forward(3)

    @pl.loop(0, 9)
    def _(k):
        rows = lax.broadcasted_iota(jnp.int32, (128, D), 0) + k * 128
        perm[slab(k, 128), :] = jnp.where(rows == order[...], 1.0, 0.0).astype(BF)

    for k in range(2):
        net.wait(("im", k))

    @pl.loop(0, 4)
    def _(r):
        xhat, _ = ln_stats(xin[slab(r, 64), :].astype(F32))
        unit[slab(r, 64), :] = (xhat * gain).astype(BF)

    def permute_normed(cols):
        npm[:, cols] = jnp.dot(unit[...], perm[:, cols], preferred_element_type=F32).astype(BF)

    column_loop(permute_normed)

    ring_oz.forward(4)

    def pack_ox(cols):
        pack_z = pack_matrix(NZ, 48, 288, 4 * OWN)
        ox[ring_ox.own(), cols] = jnp.dot(pack_z, oz[:, cols], preferred_element_type=F32).astype(BF)

    column_loop(pack_ox)
    ring_ox.start()
    ring_hz.forward(1)
    ring_hz.forward(2)
    ring_ox.forward(1)
    ring_hz.forward(3)
    ring_hz.forward(4)

    def hidden(cols):
        v = jnp.dot(npm[...], hz[:, cols], preferred_element_type=F32)
        preact[:, cols] = v
        act[:, cols] = (0.5 * v * (1.0 + jnp.tanh(GELU_C * (v + GELU_A * (v * v * v))))).astype(BF)

    column_loop(hidden)
    ring_ox.forward(2)

    def head_terms(cols):
        part[:, cols] = contract_last(act[...], ox[cols, :])

    column_loop(head_terms)

    own_rows = slab(c, 128)
    other_rows = slab(1 - c, 128)

    def swap(n, src, dst, device, comes=None):
        def copy(src, dst):
            return remote(src, dst, sw_ss.at[n], sw_rs.at[n], device)

        net.start(copy(src, dst), n, comes is not None and copy(comes, comes))

    def core_sum(n, k):
        cs[slab(k, 128), :] = part[other_rows, :].astype(BF)
        swap(n, cs.at[slab(k, 128)], cr.at[slab(k, 128)], core)
        net.wait(n)
        accb[...] = part[own_rows, :] + cr[slab(k, 128), :].astype(F32)

    core_sum(0, 0)
    es[slab(0, 128), :] = accb[...].astype(BF)
    swap(1, es.at[slab(0, 128)], er.at[slab(0, 128)], pair)

    def gelu_slope(cols):
        v = preact[:, cols]
        th = jnp.tanh(GELU_C * (v + GELU_A * (v * v * v)))
        inner = GELU_C * (1.0 + (3.0 * GELU_A) * (v * v))
        dgel[:, cols] = 0.5 * (1.0 + th) + 0.5 * v * (1.0 - th * th) * inner

    column_loop(gelu_slope)
    net.wait(1)

    @pl.loop(0, 2)
    def _(b):
        rows = slab(b, 64)
        out = xin[slab(2 * c + b, 64), :].astype(F32) + accb[rows, :] + er[rows, :].astype(F32)
        norm = jnp.sqrt(jnp.sum(out * out, axis=1, keepdims=True) + EPS)
        out = out / norm
        head[rows, :] = out
        inorm[rows, :] = jnp.broadcast_to(norm, (64, 128))
        unit[slab(2 * c + b, 64), :] = out.astype(BF)

    swap(2, unit.at[own_rows], unit.at[own_rows], core, unit.at[other_rows])
    net.wait("tx")
    net.wait(2)

    own_quarter = 2 * h

    def slope(dots, row, col):
        block = lax.shift_right_logical(row, 6) & 1
        scored = (col >= block * 64) & (col < 512 + block * 64)
        match = (col == 256 + block * 64 + (row & 63)) & (lax.shift_right_logical(row, 7) + own_quarter == q)
        value = jax.nn.sigmoid(SCALE_LOGIT * dots + BIAS_LOGIT) - jnp.where(match, 1.0, 0.0)
        return jnp.where(scored, SCALE_LOGIT * value, 0.0).astype(BF)

    @pl.loop(0, 5)
    def _(k):
        cols = slab(k, 128)
        row = lax.broadcasted_iota(jnp.int32, (256, 128), 0)
        col = lax.broadcasted_iota(jnp.int32, (256, 128), 1) + k * 128
        slopes[:, cols] = slope(contract_last(unit[...], texts[cols, :]), row, col)

    def to_image(cols):
        part[:, cols] = jnp.dot(slopes[...], texts[:, cols], preferred_element_type=F32)

    column_loop(to_image)
    core_sum(3, 1)
    es[slab(1, 128), :] = accb[...].astype(BF)
    swap(4, es.at[slab(1, 128)], er.at[slab(1, 128)], pair)

    @pl.loop(0, 5)
    def _(k):
        rows = slab(k, 128)
        row = lax.broadcasted_iota(jnp.int32, (128, 256), 1)
        col = lax.broadcasted_iota(jnp.int32, (128, 256), 0) + k * 128
        slopes_t[rows, :] = slope(contract_last(texts[rows, :], unit[...]), row, col)

    def to_text(cols):
        tgs[:, cols] = jnp.dot(slopes_t[...], unit[:, cols], preferred_element_type=F32).astype(BF)

    column_loop(to_text)
    net.wait(4)

    @pl.loop(0, 2)
    def _(b):
        rows = slab(b, 64)
        g = accb[rows, :] + er[pl.ds(pl.multiple_of(128 + b * 64, 64), 64), :].astype(F32)
        f = head[rows, :]
        out = (g - f * jnp.sum(f * g, axis=1, keepdims=True)) / inorm[rows, 0:1]
        gout[rows, :] = out
        gob[slab(2 * c + b, 64), :] = out.astype(BF)

    swap(5, gob.at[own_rows], gob.at[own_rows], core, gob.at[other_rows])

    def gz_each(pick, act):
        for k in range(2):
            for d, device, buf in ((0, last, from_next), (1, after, from_last)):
                for r in range(NLO):
                    j = 8 * d + r - 2 * k
                    if 0 <= j <= 8 and pick(r):

                        @pl.when(kk == k)
                        def _():
                            there = buf.at[pl.ds(64 * r, 64)]
                            act(remote(tgs.at[pl.ds(64 * j, 64)], there, gz_ss.at[d, r], gz_rs.at[d, r], device))

    gz_each(lambda r: True, lambda copy: copy.start())
    net.sends.append(lambda: gz_each(lambda r: True, lambda copy: copy.wait_send()))
    for r in range(NLO):
        net.arrivals["gz", r] = lambda r=r: gz_each(lambda k: k == r, lambda copy: copy.wait_recv())

    def tg_copy(r):
        return remote(
            tgy.at[pl.ds(64 * r, 64)], tgr.at[slab(y // 2, 64)], tg_ss.at[r], tg_rs.at[y // 2], ring_y(holders[r])
        )

    def tg_send(r):
        net.wait(("gz", r))
        rows = pl.ds(64 * r, 64)
        own = tgs[slab(4 + r - 2 * kk, 64), :].astype(F32)
        total = (own + from_next[rows, :].astype(F32) + from_last[rows, :].astype(F32)).astype(BF)
        tgy[rows, :] = total

        @pl.when(other(holders[r]))
        def _():
            tg_copy(r).start()

        @pl.when(holders[r] == y)
        def _():
            tgr[slab(y // 2, 64), :] = total

    def tg_sent():
        for r in range(NLO):

            @pl.when(other(holders[r]))
            def _():
                tg_copy(r).wait_send()

    def tg_wait():
        for i in range(4):

            @pl.when(other(takers[i]))
            def _():
                remote(
                    tgy.at[pl.ds(0, 64)], tgr.at[pl.ds(64 * i, 64)], tg_ss.at[0], tg_rs.at[i], pair
                ).wait_recv()

    net.wait(5)

    def hidden_back(cols):
        g = jnp.dot(gob[...], ox[:, cols], preferred_element_type=F32)
        gpre[:, cols] = (g * dgel[:, cols]).astype(BF)

    column_loop(hidden_back)
    for r in range(NLO):
        tg_send(r)
    net.sends.append(tg_sent)
    net.arrivals["tg"] = tg_wait

    def normed_terms(cols):
        part[:, cols] = contract_last(gpre[...], hz[cols, :])

    column_loop(normed_terms)
    core_sum(6, 2)
    es[pl.ds(256, 64), :] = accb[slab(1 - p, 64), :].astype(BF)
    swap(7, es.at[pl.ds(256, 64)], er.at[pl.ds(256, 64)], pair)
    xhat, rdev = ln_stats(xin[slab(2 * c + p, 64), :].astype(F32))
    net.wait(7)
    total = accb[slab(p, 64), :] + er[pl.ds(256, 64), :].astype(F32)
    high = total.astype(BF)
    low = (total - high.astype(F32)).astype(BF)

    @pl.loop(0, 3)
    def _(k):
        cols = pl.ds(pl.multiple_of(k * 384, 128), 384)
        gnat[:, cols] = contract_last(high, perm[cols, :]) + contract_last(low, perm[cols, :])

    g = gnat[...] * gain
    mean_g = jnp.sum(g, axis=1, keepdims=True) * (1.0 / D)
    mean_gx = jnp.sum(g * xhat, axis=1, keepdims=True) * (1.0 / D)
    done = slab(2 * h + c, 64)
    out_img[done, :] = (gout[slab(p, 64), :] + rdev * (g - mean_g - xhat * mean_gx)).astype(BF)
    from_far, from_core, from_both = slab(2 * (1 - h) + c, 64), slab(2 * h + 1 - c, 64), slab(2 * (1 - h) + 1 - c, 64)
    swap(8, out_img.at[done], out_img.at[done], far, out_img.at[from_far])
    swap(9, out_img.at[done], out_img.at[done], core, out_img.at[from_core])

    net.wait("tg")
    g = tgr[pl.ds(0, 64), :].astype(F32)
    for k in range(1, 4):
        g = g + tgr[slab(k, 64), :].astype(F32)
    tx = text[...].astype(F32)
    text_norm = jnp.sqrt(jnp.sum(tx * tx, axis=1, keepdims=True) + EPS)
    text_f = tx / text_norm
    out_text[...] = (g - text_f * jnp.sum(text_f * g, axis=1, keepdims=True)) / text_norm
    net.wait(8)
    swap(10, out_img.at[from_far], out_img.at[from_far], core, out_img.at[from_both])


def kernel(*refs):
    net = Net()
    stages(net, *refs)
    net.drain()


def feature_order():
    z, x, j = np.meshgrid(np.arange(NZ), np.arange(NX), np.arange(NLO * OWN), indexing="ij")
    return (x * (NZ * NLO * OWN) + z * (NLO * OWN) + j).reshape(1, D).astype(np.int32)


def shards(images, layer_norm_gain, hidden_weight, output_weight, text):

    def vm(rows, cols, kind=BF):
        return pltpu.VMEM((rows, cols), kind)

    dma = pltpu.SemaphoreType.DMA
    scratch = [
        vm(16, FW), vm(16, FW), vm(64, FW), vm(64, FW), vm(192, FW), vm(D, FW), vm(384, FW), vm(D, FW),
        vm(256, D), vm(D, D), vm(256, D), vm(256, FW), vm(256, FW, F32), vm(256, FW, F32), vm(256, D, F32),
        vm(384, D), vm(384, D), vm(320, D), vm(320, D),
        vm(256, D), vm(128, D, F32), vm(128, 128, F32), vm(128, D, F32), vm(256, D), vm(256, FW),
        vm(640, D), vm(192, D), vm(640, D), vm(256, D), vm(256, D), vm(256, D), vm(256, D), vm(256, 640), vm(640, 256), vm(128, D, F32), vm(64, D, F32),
        dma((2, 4)), dma((2, 4)), dma((2,)), dma((2,)),
        dma((2, 2, 2)), dma((2, 2, 2)), dma((4, 2, 4)), dma((4, 2, 4)),
        dma((4, 2, 2)), dma((4, 2, 2)), dma((2, 2, 4)), dma((2, 2, 4)),
        dma((2,)), dma((2,)), dma((4, 3)), dma((9,)), dma((2, 4)), dma((2, 4)), dma((4,)), dma((4,)), dma((11,)), dma((11,)),
    ]
    vmem = pl.BlockSpec(memory_space=pltpu.VMEM)
    images_gradient, grad_text = pl.pallas_call(
        kernel,
        out_shape=(jax.ShapeDtypeStruct((256, D), BF), jax.ShapeDtypeStruct((64, D), F32)),
        in_specs=[vmem] * 6,
        out_specs=(vmem, vmem),
        scratch_shapes=scratch,
        compiler_params=pltpu.CompilerParams(
            collective_id=0, has_side_effects=True, vmem_limit_bytes=56 * 2**20
        ),
        cost_estimate=pl.CostEstimate(flops=4 * 10**9, bytes_accessed=4 * 10**6, transcendentals=10**6),
    )(images, layer_norm_gain, hidden_weight, output_weight, text, jnp.asarray(feature_order()))
    return images_gradient.astype(F32), grad_text


def solution(mesh):
    placed = (P("dp", None), P(), P("dp", "tensor"), P("tensor", "dp"), P(("dp", "tensor"), None))
    return jax.shard_map(
        shards,
        mesh=mesh,
        in_specs=placed,
        out_specs=(P("dp", None), P(("dp", "tensor"), None)),
        check_vma=False,
    )
```

```python
import jax
import jax.numpy as jnp
import numpy as np
from jax import lax
from jax.experimental import pallas as pl
from jax.experimental.pallas import tpu as pltpu
from jax.sharding import PartitionSpec as P

SCALE_LOGIT = 10.0
BIAS_LOGIT = -3.0
EPS = 1e-06

NX, NZ, NY, NLO = 4, 8, 8, 4
D = 1152
FW = 1152
MAIN, REST = 32, 4
FOLDS = ((0, 640), (640, 512), (1152, 640), (1792, 512))
OWN = 9
ARRIVALS = (
    ("Az", 0, 1), ("Bx", 0, 1), ("Bz", 0, 1), ("Ax", 0, 1), ("Bx", 0, 2), ("Az", 0, 2), ("Bx", -1, 1), ("Bz", 0, 2),
    ("Az", -1, 1), ("Bx", 1, 1), ("Ax", 0, 2), ("Az", 1, 1), ("Bx", -1, 2), ("Az", 0, 3), ("Bx", -2, 1), ("Bz", 0, 3),
    ("Bx", 2, 1), ("Az", -1, 2), ("Bx", 1, 2), ("Bx", -2, 2), ("Az", 2, 1), ("Az", 1, 2), ("Bx", -3, 1), ("Az", 0, 4),
    ("Bz", 0, 4), ("Bx", 3, 1), ("Bx", 2, 2), ("Az", -1, 3), ("Bx", -3, 2), ("Az", 2, 2), ("Bx", 4, 1), ("Az", 1, 3),
    ("Bx", 3, 2), ("Az", -1, 4), ("Bx", 4, 2), ("Az", 2, 3), ("Az", 1, 4), ("Az", 2, 4),
)
MESH = pl.DeviceIdType.MESH
BF = jnp.bfloat16
F32 = jnp.float32
GELU_C = 0.7978845608028654
GELU_A = 0.044715


def contract_last(left, right):
    return lax.dot_general(left, right, (((1,), (1,)), ((), ())), preferred_element_type=F32)


def ident(x, z, y, c):
    return (x * (NZ * NLO) + z * NLO + lax.rem(y, NLO), (y // NLO) * 2 + c)


class Net:
    def __init__(self):
        self.sends, self.arrivals = [], {}

    def start(self, copy, name, arrival=None):
        copy.start()
        self.sends.append(copy.wait_send)
        self.arrivals[name] = (arrival or copy).wait_recv

    def wait(self, name):
        self.arrivals.pop(name)()

    def drain(self):
        for name in list(self.arrivals):
            self.wait(name)
        for wait_send in self.sends:
            wait_send()


class Ring:
    def __init__(self, net, buf, rows, size, pos, at, peers, sems, last):
        self.net, self.buf, self.rows, self.size, self.pos, self.at = net, buf, rows, size, pos, at
        self.peers, self.sems, self.last = peers, sems, last
        self.steps = size // 2

    def part(self, step, way):
        if step < self.steps:
            return 0, self.rows
        if self.last is None:
            return way * (self.rows // 2), self.rows // 2
        return (0, self.rows) if way == self.last else None

    def copy(self, step, way, back):
        slot = lax.rem(self.pos + (-back if way == 0 else back) + 2 * self.size, self.size)
        off, rows = self.part(step, way)
        ref = self.buf.at[pl.ds(pl.multiple_of(self.at(slot) + off, 16), rows)]
        ssem, rsem = self.sems(step - 1, way)
        return pltpu.make_async_remote_copy(
            src_ref=ref, dst_ref=ref, send_sem=ssem, recv_sem=rsem, device_id=self.peers[way], device_id_type=MESH
        )

    def send(self, step):
        for way in (0, 1):
            if self.part(step, way):
                self.go(step, way)

    def go(self, step, way):
        self.net.start(self.copy(step, way, step - 1), (self, step, way), self.copy(step, way, step))

    def forward(self, step):
        for way in (0, 1):
            if self.part(step, way):
                self.net.wait((self, step, way))
                if step < self.steps and self.part(step + 1, way):
                    self.go(step + 1, way)


def pick_matrix(rows, cols, pairs):
    row = lax.broadcasted_iota(jnp.int32, (rows, cols), 0)
    col = lax.broadcasted_iota(jnp.int32, (rows, cols), 1)
    hit = jnp.zeros((rows, cols), F32)
    for test in pairs:
        hit = jnp.where(test(row, col), 1.0, hit)
    return hit.astype(BF)


def column_loop(body):
    @pl.loop(0, 3)
    def _(k):
        body(pl.ds(pl.multiple_of(k * 384, 128), 384))


def ln_stats(v):
    v = v - jnp.sum(v, axis=1, keepdims=True) * (1.0 / D)
    var = jnp.sum(v * v, axis=1, keepdims=True) * (1.0 / D)
    rdev = 1.0 / jnp.sqrt(var + EPS)
    return v * rdev, rdev


def stages(
    net, images, gain_in, h_in, o_in, text, order,
    out_img, out_text,
    w_own, wy, hm, om, rest, xin, xp, perm, npm, gperm, act, preact, dgel, part,
    cs, cr, es, er, unit, head, inorm, gout, gob, gpre, texts, tz, tgs, from_next, from_last, tgy, tgr, slopes, slopes_t, accb, tp,
    y_ss, y_rs, im_ss, im_rs, ax_ss, ax_rs, az_ss, az_rs, bz_ss, bz_rs, bx_ss, bx_rs,
    tz_ss, tz_rs, tx_ss, tx_rs, gz_ss, gz_rs, tg_ss, tg_rs, sw_ss, sw_rs,
):
    a = lax.axis_index("dp")
    t = lax.axis_index("tensor")
    x, z, lo = a // (NZ * NLO), lax.rem(a // NLO, NZ), lax.rem(a, NLO)
    h, c = t // 2, lax.rem(t, 2)
    y = h * NLO + lo
    p = lax.rem(lo, 2)
    q = p * 2 + c
    kk = lo // 2
    n_dp = NX * NZ * NLO
    mine = p == h

    core = ident(x, z, y, 1 - c)
    pair = ident(x, z, y + 1 - 2 * p, c)
    far = ident(x, z, lax.rem(y + NLO, NY), c)
    x_up = ident(lax.rem(x + 1, NX), z, y, c)
    x_dn = ident(lax.rem(x + NX - 1, NX), z, y, c)
    z_up = ident(x, lax.rem(z + 1, NZ), y, c)
    z_dn = ident(x, lax.rem(z + NZ - 1, NZ), y, c)

    last = (lax.rem(a - NLO + n_dp, n_dp), t)
    after = (lax.rem(a + NLO, n_dp), t)

    def ring_y(k):
        return ident(x, z, k, c)

    def when(*conditions):
        live = [k for k in conditions if not isinstance(k, bool)]
        if not all(k for k in conditions if isinstance(k, bool)):
            return lambda body: None
        if not live:
            return lambda body: body()
        both = live[0]
        for k in live[1:]:
            both = both & k
        return pl.when(both)

    takers = [h + 2 * i for i in range(4)]
    holders = [4 * p + l for l in range(NLO)]

    def other(k):
        return jnp.logical_not(k == y)

    def remote(src, dst, ss, rs, device):
        return pltpu.make_async_remote_copy(
            src_ref=src, dst_ref=dst, send_sem=ss, recv_sem=rs, device_id=device, device_id_type=MESH
        )

    def slab(k, rows):
        return pl.ds(k * rows if isinstance(k, int) else pl.multiple_of(k * rows, rows), rows)

    from_next[...] = jnp.zeros((256, D), BF)
    from_last[...] = jnp.zeros((256, D), BF)
    width = h_in.shape[1]
    turn = pick_matrix(16, OWN, [lambda row, col: row == col])
    w_own[...] = jnp.zeros((16, 2 * FW), BF)
    w_own[pl.ds(0, OWN), pl.ds(0, width)] = h_in[...]
    w_own[:, pl.ds(FW, width)] = contract_last(turn, o_in[...]).astype(BF)

    bar = pltpu.get_barrier_semaphore()

    def signal(device):
        pl.semaphore_signal(bar, inc=1, device_id=device, device_id_type=MESH)

    for device in (core, pair, far, x_up, x_dn, z_up, z_dn, last, after):
        signal(device)
    for k in takers + holders:

        @pl.when(other(k))
        def _():
            signal(ring_y(k))

    pl.semaphore_wait(bar, 17 - 2 * mine.astype(jnp.int32))

    def y_copy(i):
        return remote(w_own, wy.at[slab(lo, 16)], y_ss.at[i], y_rs.at[lo], ring_y(takers[i]))

    def y_sent():
        for i in range(4):

            @pl.when(other(takers[i]))
            def _():
                y_copy(i).wait_send()

    def y_wait():
        for l in range(NLO):

            @pl.when(other(holders[l]))
            def _():
                remote(w_own, wy.at[slab(l, 16)], y_ss.at[0], y_rs.at[l], pair).wait_recv()

    for i in range(4):

        @pl.when(other(takers[i]))
        def _():
            y_copy(i).start()

        @pl.when(takers[i] == y)
        def _():
            wy[slab(lo, 16), :] = w_own[...]

    net.sends.append(y_sent)
    net.arrivals["y"] = y_wait

    @pl.loop(0, 9)
    def _(k):
        rows = lax.broadcasted_iota(jnp.int32, (128, D), 0) + k * 128
        perm[slab(k, 128), :] = jnp.where(rows == order[...], 1.0, 0.0).astype(BF)

    gain = gain_in[...].reshape(1, D)
    high = gain.astype(BF)
    middle = (gain - high.astype(F32)).astype(BF)
    low = (gain - high.astype(F32) - middle.astype(F32)).astype(BF)
    three = jnp.concatenate([high, middle, low, jnp.zeros((13, D), BF)], axis=0)

    def permute_text(cols):
        terms = jnp.dot(three, perm[:, cols], preferred_element_type=F32)
        gperm[:, cols] = jnp.sum(terms, axis=0, keepdims=True)
        tp[:, cols] = jnp.dot(text[...], perm[:, cols], preferred_element_type=F32).astype(BF)

    column_loop(permute_text)

    tx = tp[...].astype(F32)
    text_norm = jnp.sqrt(jnp.sum(tx * tx, axis=1, keepdims=True) + EPS)
    tz[pl.ds(64, 64), :] = (tx / text_norm).astype(BF)
    for d, (device, back) in enumerate(((after, last), (last, after))):
        mine_tz, there, here = tz.at[pl.ds(64, 64)], tz.at[pl.ds(128 * d, 64)], tz.at[pl.ds(128 * d, 64)]
        net.start(
            remote(mine_tz, there, tz_ss.at[d], tz_rs.at[d], device), ("tz", d),
            remote(mine_tz, here, tz_ss.at[d], tz_rs.at[d], back),
        )

    def text_slot(i, d):
        k = i % 2
        used = {(0, 2): lo == 0, (1, 0): lo >= 2, (1, 2): lo <= 2}.get((k, d), True)
        return 4 * d + lo - 2 * k, used

    def tx_copy(i, d):
        j, _ = text_slot(i, d)
        return remote(
            tz.at[pl.ds(64 * d, 64)], texts.at[slab(j, 64)], tx_ss.at[i, d], tx_rs.at[j], ring_y(takers[i])
        )

    def tx_send(i, d):
        j, used = text_slot(i, d)

        @when(used, other(takers[i]))
        def _():
            tx_copy(i, d).start()

        @when(used, takers[i] == y)
        def _():
            texts[slab(j, 64), :] = tz[pl.ds(64 * d, 64), :]

    def tx_sent():
        for d in range(3):
            for i in range(4):

                @when(text_slot(i, d)[1], other(takers[i]))
                def _():
                    tx_copy(i, d).wait_send()

    def tx_wait():
        for j in range(9):

            @when(jnp.logical_not(mine & (p == j % 4)))
            def _():
                remote(
                    tz.at[pl.ds(64, 64)], texts.at[slab(j, 64)], tx_ss.at[0, 0], tx_rs.at[j], pair
                ).wait_recv()

    net.sends.append(tx_sent)
    net.arrivals["tx"] = tx_wait
    texts[slab(9, 64), :] = jnp.zeros((64, D), BF)

    def place(x_at, z_at, rows):
        return (x_at * NZ + z_at) * rows

    def x_of(rel):
        return lax.rem(x + rel + NX, NX)

    def z_of(rel):
        return lax.rem(z + rel + NZ, NZ)

    rings = {}

    def ring(key, buf, rows, size, pos, at, peers, ss, rs, last):
        rings.setdefault(key, []).append(
            Ring(net, buf, rows, size, pos, at, peers, lambda step, way: (ss.at[step, way], rs.at[step, way]), last)
        )

    ups, zs = (x_up, x_dn), (z_up, z_dn)
    ring(("Ax", 0), hm, MAIN, NX, x, lambda k: place(k, z, MAIN), ups, ax_ss, ax_rs, None)
    for n, rel in enumerate((0, -1, 1, 2)):
        ring(
            ("Az", rel), hm, MAIN, NZ, z, lambda k, rel=rel: place(x_of(rel), k, MAIN), zs,
            az_ss.at[n], az_rs.at[n], None,
        )
    for n, (buf, rows) in enumerate(((om, MAIN), (rest, 16))):
        ring(
            ("Bz", 0), buf, rows, NZ, z, lambda k, rows=rows: place(x, k, rows), zs,
            bz_ss.at[n], bz_rs.at[n], 0 if n else None,
        )
        for m, rel in enumerate((0, -1, 1, -2, 2, -3, 3, 4)):
            ring(
                ("Bx", rel), buf, rows, NX, x, lambda k, rel=rel, rows=rows: place(k, z_of(rel), rows), ups,
                bx_ss.at[n, m], bx_rs.at[n, m], m % 2 if n else None,
            )

    def begin(key):
        for one in rings[key]:
            one.send(1)

    net.wait("y")
    keep = pick_matrix(MAIN, 64, [lambda row, col: row == lax.shift_right_logical(col, 4) * OWN + (col & 15)])
    keep = jnp.where((lax.broadcasted_iota(jnp.int32, (MAIN, 64), 1) & 15) < OWN, keep, jnp.zeros_like(keep))
    mine_main = pl.ds(pl.multiple_of(place(x, z, MAIN), MAIN), MAIN)
    hm[mine_main, :] = jnp.dot(keep, wy[:, pl.ds(0, FW)], preferred_element_type=F32).astype(BF)
    begin(("Az", 0))
    om[mine_main, :] = jnp.dot(keep, wy[:, pl.ds(FW, FW)], preferred_element_type=F32).astype(BF)
    folded = jnp.zeros((16, 640), F32)
    for u, (lane, lanes) in enumerate(FOLDS):
        pick = pick_matrix(16, 64, [lambda row, col: ((row & 3) == u) & (col == 48 + 5 + lax.shift_right_logical(row, 2))])
        got = jnp.dot(pick, wy[:, pl.ds(lane, lanes)], preferred_element_type=F32)
        if lanes < 640:
            got = jnp.concatenate([got, jnp.zeros((16, 640 - lanes), F32)], axis=1)
        folded = folded + got
    rest[pl.ds(pl.multiple_of(place(x, z, 16), 16), 16), :] = folded.astype(BF)
    for key in (("Bz", 0), ("Bx", 0), ("Ax", 0)):
        begin(key)

    def im_copy(k, block):
        return remote(
            images.at[slab(2 * h + k, 64)], xin.at[slab(2 * k + block, 64)], im_ss.at[k], im_rs.at[k], pair
        )

    for k in range(2):
        net.start(im_copy(k, p), ("im", k), im_copy(k, 1 - p))
        xin[slab(2 * k + p, 64), :] = images[slab(2 * h + k, 64), :]

    sends = [lambda i=i: tx_send(i, 1) for i in range(4)]
    sends += [lambda: net.wait(("tz", 0)), lambda: net.wait(("tz", 1))]
    sends += [lambda i=i, d=d: tx_send(i, d) for d in (0, 2) for i in range(4)]

    def normed_rows():
        for k in range(2):
            net.wait(("im", k))

        def permute_images(cols):
            xp[:, cols] = jnp.dot(xin[...], perm[:, cols], preferred_element_type=F32).astype(BF)

        column_loop(permute_images)

        @pl.loop(0, 4)
        def _(r):
            xhat, _ = ln_stats(xp[slab(r, 64), :].astype(F32))
            npm[slab(r, 64), :] = (xhat * gperm[...]).astype(BF)

    for n, (route, rel, step) in enumerate(ARRIVALS):
        for one in rings[route, rel]:
            one.forward(step)
        if route == "Ax":
            for k in ((-1, 1), (2,))[step - 1]:
                begin(("Az", k))
        if route == "Bz":
            for k in (-step, step) if step < 4 else (4,):
                begin(("Bx", k))
        if n % 2 == 0 and sends:
            sends.pop(0)()
        if n == 30:
            normed_rows()

    def unfold(u, buf, lane, lanes):
        tests = [lambda row, col: col == lax.shift_right_logical(row, 2) * 16 + (row & 3) * 4 + u]
        got = jnp.dot(pick_matrix(128, 512, tests), rest[:, pl.ds(0, lanes)], preferred_element_type=F32)
        buf[pl.ds(1024, 128), pl.ds(lane, lanes)] = got.astype(BF)

    for u, (lane, lanes) in enumerate(FOLDS):
        unfold(u, hm if lane < FW else om, lane % FW, lanes)

    def hidden(cols):
        v = jnp.dot(npm[...], hm[:, cols], preferred_element_type=F32)
        preact[:, cols] = v
        act[:, cols] = (0.5 * v * (1.0 + jnp.tanh(GELU_C * (v + GELU_A * (v * v * v))))).astype(BF)

    column_loop(hidden)

    def head_terms(cols):
        part[:, cols] = contract_last(act[...], om[cols, :])

    column_loop(head_terms)

    def swap(n, src, dst, device, comes=None):
        def copy(src, dst):
            return remote(src, dst, sw_ss.at[n], sw_rs.at[n], device)

        net.start(copy(src, dst), n, comes is not None and copy(comes, comes))

    def core_send(n, k, at, b):
        rows = pl.ds(128 * k + 64 * at, 64)
        cs[rows, :] = part[slab(2 * (1 - c) + b, 64), :].astype(BF)
        swap(n + at, cs.at[rows], cr.at[rows], core)

    def core_add(n, k, at, b):
        net.wait(n + at)
        rows = pl.ds(128 * k + 64 * at, 64)
        accb[slab(b, 64), :] = part[slab(2 * c + b, 64), :] + cr[rows, :].astype(F32)

    def pair_send(n, k, at, b):
        rows = pl.ds(128 * k + 64 * at, 64)
        es[rows, :] = accb[slab(b, 64), :].astype(BF)
        swap(n + at, es.at[rows], er.at[rows], pair)

    def sum_start(n, k):
        for b in range(2):
            core_send(n, k, b, b)
        for b in range(2):
            core_add(n, k, b, b)
            pair_send(n + 2, k, b, b)

    def sum_end(n, k, b):
        net.wait(n + 2 + b)
        return accb[slab(b, 64), :] + er[pl.ds(128 * k + 64 * b, 64), :].astype(F32)

    def share(n, ref, b):
        rows, comes = slab(2 * c + b, 64), slab(2 * (1 - c) + b, 64)
        swap(n + b, ref.at[rows], ref.at[rows], core, ref.at[comes])

    sum_start(0, 0)

    def gelu_slope(cols):
        v = preact[:, cols]
        th = jnp.tanh(GELU_C * (v + GELU_A * (v * v * v)))
        inner = GELU_C * (1.0 + (3.0 * GELU_A) * (v * v))
        dgel[:, cols] = 0.5 * (1.0 + th) + 0.5 * v * (1.0 - th * th) * inner

    column_loop(gelu_slope)
    for b in range(2):
        rows = slab(b, 64)
        out = xp[slab(2 * c + b, 64), :].astype(F32) + sum_end(0, 0, b)
        norm = jnp.sqrt(jnp.sum(out * out, axis=1, keepdims=True) + EPS)
        out = out / norm
        head[rows, :] = out
        inorm[rows, :] = jnp.broadcast_to(norm, (64, 128))
        unit[slab(2 * c + b, 64), :] = out.astype(BF)
        share(4, unit, b)
    net.wait("tx")
    for b in range(2):
        net.wait(4 + b)

    own_quarter = 2 * h

    def slope(dots, row, col):
        block = lax.shift_right_logical(row, 6) & 1
        scored = (col >= block * 64) & (col < 512 + block * 64)
        match = (col == 256 + block * 64 + (row & 63)) & (lax.shift_right_logical(row, 7) + own_quarter == q)
        value = jax.nn.sigmoid(SCALE_LOGIT * dots + BIAS_LOGIT) - jnp.where(match, 1.0, 0.0)
        return jnp.where(scored, SCALE_LOGIT * value, 0.0).astype(BF)

    @pl.loop(0, 5)
    def _(k):
        cols = slab(k, 128)
        row = lax.broadcasted_iota(jnp.int32, (256, 128), 0)
        col = lax.broadcasted_iota(jnp.int32, (256, 128), 1) + k * 128
        slopes[:, cols] = slope(contract_last(unit[...], texts[cols, :]), row, col)

    def to_image(cols):
        part[:, cols] = jnp.dot(slopes[...], texts[:, cols], preferred_element_type=F32)

    column_loop(to_image)
    sum_start(6, 1)

    @pl.loop(0, 5)
    def _(k):
        rows = slab(k, 128)
        row = lax.broadcasted_iota(jnp.int32, (128, 256), 1)
        col = lax.broadcasted_iota(jnp.int32, (128, 256), 0) + k * 128
        slopes_t[rows, :] = slope(contract_last(texts[rows, :], unit[...]), row, col)

    def to_text(cols):
        tgs[:, cols] = jnp.dot(slopes_t[...], unit[:, cols], preferred_element_type=F32).astype(BF)

    column_loop(to_text)
    def gz_each(pick, act):
        for k in range(2):
            for d, device, buf in ((0, last, from_next), (1, after, from_last)):
                for r in range(NLO):
                    j = 8 * d + r - 2 * k
                    if 0 <= j <= 8 and pick(r):

                        @pl.when(kk == k)
                        def _():
                            there = buf.at[pl.ds(64 * r, 64)]
                            act(remote(tgs.at[pl.ds(64 * j, 64)], there, gz_ss.at[d, r], gz_rs.at[d, r], device))

    gz_each(lambda r: True, lambda copy: copy.start())
    net.sends.append(lambda: gz_each(lambda r: True, lambda copy: copy.wait_send()))
    for r in range(NLO):
        net.arrivals["gz", r] = lambda r=r: gz_each(lambda k: k == r, lambda copy: copy.wait_recv())

    for b in range(2):
        rows = slab(b, 64)
        g = sum_end(6, 1, b)
        f = head[rows, :]
        out = (g - f * jnp.sum(f * g, axis=1, keepdims=True)) / inorm[rows, 0:1]
        gout[rows, :] = out
        gob[slab(2 * c + b, 64), :] = out.astype(BF)
        share(10, gob, b)

    def tg_copy(r):
        return remote(
            tgy.at[pl.ds(64 * r, 64)], tgr.at[slab(y // 2, 64)], tg_ss.at[r], tg_rs.at[y // 2], ring_y(holders[r])
        )

    def tg_send(r):
        net.wait(("gz", r))
        rows = pl.ds(64 * r, 64)
        own = tgs[slab(4 + r - 2 * kk, 64), :].astype(F32)
        total = (own + from_next[rows, :].astype(F32) + from_last[rows, :].astype(F32)).astype(BF)
        tgy[rows, :] = total

        @pl.when(other(holders[r]))
        def _():
            tg_copy(r).start()

        @pl.when(holders[r] == y)
        def _():
            tgr[slab(y // 2, 64), :] = total

    def tg_sent():
        for r in range(NLO):

            @pl.when(other(holders[r]))
            def _():
                tg_copy(r).wait_send()

    def tg_wait():
        for i in range(4):

            @pl.when(other(takers[i]))
            def _():
                remote(
                    tgy.at[pl.ds(0, 64)], tgr.at[pl.ds(64 * i, 64)], tg_ss.at[0], tg_rs.at[i], pair
                ).wait_recv()

    net.sends.append(tg_sent)
    net.arrivals["tg"] = tg_wait
    tg_send(0)
    for b in range(2):
        net.wait(10 + b)

    def hidden_back(cols):
        g = jnp.dot(gob[...], om[:, cols], preferred_element_type=F32)
        gpre[:, cols] = (g * dgel[:, cols]).astype(BF)

    column_loop(hidden_back)
    tg_send(1)

    def normed_terms(cols):
        part[:, cols] = contract_last(gpre[...], hm[cols, :])

    column_loop(normed_terms)
    core_send(12, 2, 0, 1 - p)
    core_send(12, 2, 1, p)
    core_add(12, 2, 0, 1 - p)
    pair_send(14, 2, 0, 1 - p)
    core_add(12, 2, 1, p)
    tg_send(2)
    tg_send(3)
    xhat, rdev = ln_stats(xp[slab(2 * c + p, 64), :].astype(F32))
    net.wait(14)
    g = (accb[slab(p, 64), :] + er[pl.ds(256, 64), :].astype(F32)) * gperm[...]
    mean_g = jnp.sum(g, axis=1, keepdims=True) * (1.0 / D)
    mean_gx = jnp.sum(g * xhat, axis=1, keepdims=True) * (1.0 / D)
    done = slab(2 * h + c, 64)
    result = (gout[slab(p, 64), :] + rdev * (g - mean_g - xhat * mean_gx)).astype(BF)

    def natural_image(cols):
        out_img[done, cols] = contract_last(result, perm[cols, :]).astype(BF)

    column_loop(natural_image)
    from_far, from_core, from_both = slab(2 * (1 - h) + c, 64), slab(2 * h + 1 - c, 64), slab(2 * (1 - h) + 1 - c, 64)
    swap(15, out_img.at[done], out_img.at[done], far, out_img.at[from_far])
    swap(16, out_img.at[done], out_img.at[done], core, out_img.at[from_core])

    net.wait("tg")
    g = tgr[pl.ds(0, 64), :].astype(F32)
    for k in range(1, 4):
        g = g + tgr[slab(k, 64), :].astype(F32)
    tx = tp[...].astype(F32)
    text_norm = jnp.sqrt(jnp.sum(tx * tx, axis=1, keepdims=True) + EPS)
    text_f = tx / text_norm
    g = (g - text_f * jnp.sum(text_f * g, axis=1, keepdims=True)) / text_norm
    high = g.astype(BF)
    both = jnp.concatenate([high, (g - high.astype(F32)).astype(BF)], axis=0)

    def natural_text(cols):
        got = contract_last(both, perm[cols, :])
        out_text[:, cols] = got[:64] + got[64:]

    column_loop(natural_text)
    net.wait(15)
    swap(17, out_img.at[from_far], out_img.at[from_far], core, out_img.at[from_both])


def kernel(*refs):
    net = Net()
    stages(net, *refs)
    net.drain()


def feature_order():
    first = (np.arange(NX * NZ) * (MAIN + REST))[:, None]
    main = (first + np.arange(MAIN)).reshape(-1)
    rest = (first + MAIN + np.arange(REST)).reshape(-1)
    return np.concatenate([main, rest]).reshape(1, D).astype(np.int32)


def shards(images, layer_norm_gain, hidden_weight, output_weight, text):

    def vm(rows, cols, kind=BF):
        return pltpu.VMEM((rows, cols), kind)

    dma = pltpu.SemaphoreType.DMA
    scratch = [
        vm(16, 2 * FW), vm(64, 2 * FW), vm(D, FW), vm(D, FW), vm(512, 640),
        vm(256, D), vm(256, D), vm(D, D), vm(256, D), vm(1, D, F32),
        vm(256, FW), vm(256, FW, F32), vm(256, FW, F32), vm(256, D, F32),
        vm(384, D), vm(384, D), vm(320, D), vm(320, D),
        vm(256, D), vm(128, D, F32), vm(128, 128, F32), vm(128, D, F32), vm(256, D), vm(256, FW),
        vm(640, D), vm(192, D), vm(640, D), vm(256, D), vm(256, D), vm(256, D), vm(256, D), vm(256, 640), vm(640, 256), vm(128, D, F32), vm(64, D),
        dma((4,)), dma((4,)), dma((2,)), dma((2,)),
        dma((2, 2)), dma((2, 2)), dma((4, 4, 2)), dma((4, 4, 2)),
        dma((2, 4, 2)), dma((2, 4, 2)), dma((2, 8, 2, 2)), dma((2, 8, 2, 2)),
        dma((2,)), dma((2,)), dma((4, 3)), dma((9,)), dma((2, 4)), dma((2, 4)), dma((4,)), dma((4,)), dma((18,)), dma((18,)),
    ]
    vmem = pl.BlockSpec(memory_space=pltpu.VMEM)
    images_gradient, grad_text = pl.pallas_call(
        kernel,
        out_shape=(jax.ShapeDtypeStruct((256, D), BF), jax.ShapeDtypeStruct((64, D), F32)),
        in_specs=[vmem] * 6,
        out_specs=(vmem, vmem),
        scratch_shapes=scratch,
        compiler_params=pltpu.CompilerParams(
            collective_id=0, has_side_effects=True, vmem_limit_bytes=56 * 2**20
        ),
        cost_estimate=pl.CostEstimate(flops=4 * 10**9, bytes_accessed=4 * 10**6, transcendentals=10**6),
    )(images, layer_norm_gain, hidden_weight, output_weight, text, jnp.asarray(feature_order()))
    return images_gradient.astype(F32), grad_text


def solution(mesh):
    placed = (P("dp", None), P(), P("dp", "tensor"), P("tensor", "dp"), P(("dp", "tensor"), None))
    return jax.shard_map(
        shards,
        mesh=mesh,
        in_specs=placed,
        out_specs=(P("dp", None), P(("dp", "tensor"), None)),
        check_vma=False,
    )
```

```python
import jax
import jax.numpy as jnp
import numpy as np
from jax import lax
from jax.experimental import pallas as pl
from jax.experimental.pallas import tpu as pltpu
from jax.sharding import PartitionSpec as P

SCALE_LOGIT = 10.0
BIAS_LOGIT = -3.0
EPS = 1e-06

NX, NZ, NY, NLO = 4, 8, 8, 4
D = 1152
FW = 1152
MAIN, REST = 32, 4
FOLDS = ((0, 640), (640, 512), (1152, 640), (1792, 512))
OWN = 9
SPANS = ((0, FW), (FW, 256))
ARRIVALS = (
    ("Az", 0, 1), ("Bx", 0, 1), ("Bz", 0, 1), ("Ax", 0, 1), ("Bx", 0, 2), ("Az", 0, 2), ("Bx", -1, 1), ("Bz", 0, 2),
    ("Az", -1, 1), ("Bx", 1, 1), ("Ax", 0, 2), ("Az", 1, 1), ("Bx", -1, 2), ("Az", 0, 3), ("Bx", -2, 1), ("Bz", 0, 3),
    ("Bx", 2, 1), ("Az", -1, 2), ("Bx", 1, 2), ("Bx", -2, 2), ("Az", 2, 1), ("Az", 1, 2), ("Bx", -3, 1), ("Az", 0, 4),
    ("Bz", 0, 4), ("Bx", 3, 1), ("Bx", 2, 2), ("Az", -1, 3), ("Bx", -3, 2), ("Az", 2, 2), ("Bx", 4, 1), ("Az", 1, 3),
    ("Bx", 3, 2), ("Az", -1, 4), ("Bx", 4, 2), ("Az", 2, 3), ("Az", 1, 4), ("Az", 2, 4),
)
MESH = pl.DeviceIdType.MESH
BF = jnp.bfloat16
F32 = jnp.float32
GELU_C = 0.7978845608028654
GELU_A = 0.044715


def contract_last(left, right):
    return lax.dot_general(left, right, (((1,), (1,)), ((), ())), preferred_element_type=F32)


def ident(x, z, y, c):
    return (x * (NZ * NLO) + z * NLO + lax.rem(y, NLO), (y // NLO) * 2 + c)


ROUTES = {
    (0, 0): ((4,), ()),
    (0, 1): ((), (6, 4, 2)),
    (0, 2): ((2, 4, 6), ()),
    (1, 0): ((4,), (0,)),
    (1, 1): ((2,), (0, 6, 4)),
    (1, 2): ((2,), (6,)),
    (2, 0): ((), (0, 6, 4)),
    (2, 1): ((4, 6, 0), ()),
    (2, 2): ((6,), ()),
    (3, 0): ((4,), (2, 0, 6)),
    (3, 1): ((4, 6), (2, 0)),
    (4, 0): ((5,), (1,)),
    (4, 1): ((5,), (3, 1, 7)),
    (4, 2): ((5, 7), (3, 1)),
    (5, 0): ((1,), ()),
    (5, 1): ((), (3, 1, 7)),
    (5, 2): ((7,), (3,)),
    (6, 0): ((7, 1), (5, 3)),
    (6, 1): ((7, 1, 3), (5,)),
    (6, 2): ((7,), (3,)),
    (7, 0): ((1, 3), (5,)),
    (7, 1): ((1, 3), (5,)),
}


class Net:
    def __init__(self):
        self.sends, self.arrivals = [], {}

    def start(self, copy, name, arrival=None):
        copy.start()
        self.sends.append(copy.wait_send)
        self.arrivals[name] = (arrival or copy).wait_recv

    def wait(self, name):
        self.arrivals.pop(name)()

    def drain(self):
        for name in list(self.arrivals):
            self.wait(name)
        for wait_send in self.sends:
            wait_send()


class Ring:
    def __init__(self, net, buf, rows, size, pos, at, peers, sems, last):
        self.net, self.buf, self.rows, self.size, self.pos, self.at = net, buf, rows, size, pos, at
        self.peers, self.sems, self.last = peers, sems, last
        self.steps = size // 2

    def part(self, step, way):
        if step < self.steps:
            return 0, self.rows
        if self.last is None:
            return way * (self.rows // 2), self.rows // 2
        return (0, self.rows) if way == self.last else None

    def copy(self, step, way, back):
        slot = lax.rem(self.pos + (-back if way == 0 else back) + 2 * self.size, self.size)
        off, rows = self.part(step, way)
        ref = self.buf.at[pl.ds(pl.multiple_of(self.at(slot) + off, 16), rows)]
        ssem, rsem = self.sems(step - 1, way)
        return pltpu.make_async_remote_copy(
            src_ref=ref, dst_ref=ref, send_sem=ssem, recv_sem=rsem, device_id=self.peers[way], device_id_type=MESH
        )

    def send(self, step):
        for way in (0, 1):
            if self.part(step, way):
                self.go(step, way)

    def go(self, step, way):
        self.net.start(self.copy(step, way, step - 1), (self, step, way), self.copy(step, way, step))

    def forward(self, step):
        for way in (0, 1):
            if self.part(step, way):
                self.net.wait((self, step, way))
                if step < self.steps and self.part(step + 1, way):
                    self.go(step + 1, way)


def pick_matrix(rows, cols, pairs):
    row = lax.broadcasted_iota(jnp.int32, (rows, cols), 0)
    col = lax.broadcasted_iota(jnp.int32, (rows, cols), 1)
    hit = jnp.zeros((rows, cols), F32)
    for test in pairs:
        hit = jnp.where(test(row, col), 1.0, hit)
    return hit.astype(BF)


def column_loop(body):
    @pl.loop(0, 3)
    def _(k):
        body(pl.ds(pl.multiple_of(k * 384, 128), 384))


def ln_stats(v):
    v = v - jnp.sum(v, axis=1, keepdims=True) * (1.0 / D)
    var = jnp.sum(v * v, axis=1, keepdims=True) * (1.0 / D)
    rdev = 1.0 / jnp.sqrt(var + EPS)
    return v * rdev, rdev


def stages(
    net, images, gain_in, h_in, o_in, text, order,
    out_img, out_text,
    w_own, o_own, wy, wo, stack, hm, om, rest, xin, xp, perm, npm, gperm, act, preact, dgel, part,
    cs, cr, es, er, unit, head, inorm, gout, gob, gpre, texts, tz, tgs, from_next, from_last, tgy, tgr, slopes, slopes_t, accb, tp,
    y_ss, y_rs, im_ss, im_rs, ax_ss, ax_rs, az_ss, az_rs, bz_ss, bz_rs, bx_ss, bx_rs,
    tz_ss, tz_rs, tx_ss, tf_ss, tx_rs, gz_ss, gz_rs, tg_ss, tg_rs, sw_ss, sw_rs,
):
    a = lax.axis_index("dp")
    t = lax.axis_index("tensor")
    x, z, lo = a // (NZ * NLO), lax.rem(a // NLO, NZ), lax.rem(a, NLO)
    h, c = t // 2, lax.rem(t, 2)
    y = h * NLO + lo
    p = lax.rem(lo, 2)
    q = p * 2 + c
    kk = lo // 2
    n_dp = NX * NZ * NLO
    mine = p == h

    core = ident(x, z, y, 1 - c)
    pair = ident(x, z, y + 1 - 2 * p, c)
    far = ident(x, z, lax.rem(y + NLO, NY), c)
    x_up = ident(lax.rem(x + 1, NX), z, y, c)
    x_dn = ident(lax.rem(x + NX - 1, NX), z, y, c)
    z_up = ident(x, lax.rem(z + 1, NZ), y, c)
    z_dn = ident(x, lax.rem(z + NZ - 1, NZ), y, c)

    last = (lax.rem(a - NLO + n_dp, n_dp), t)
    after = (lax.rem(a + NLO, n_dp), t)

    def ring_y(k):
        return ident(x, z, k, c)

    def when(*conditions):
        live = [k for k in conditions if not isinstance(k, bool)]
        if not all(k for k in conditions if isinstance(k, bool)):
            return lambda body: None
        if not live:
            return lambda body: body()
        both = live[0]
        for k in live[1:]:
            both = both & k
        return pl.when(both)

    takers = [h + 2 * i for i in range(4)]
    holders = [4 * p + l for l in range(NLO)]

    def other(k):
        return jnp.logical_not(k == y)

    def remote(src, dst, ss, rs, device):
        return pltpu.make_async_remote_copy(
            src_ref=src, dst_ref=dst, send_sem=ss, recv_sem=rs, device_id=device, device_id_type=MESH
        )

    def slab(k, rows):
        return pl.ds(k * rows if isinstance(k, int) else pl.multiple_of(k * rows, rows), rows)

    from_next[...] = jnp.zeros((256, D), BF)
    from_last[...] = jnp.zeros((256, D), BF)
    width = h_in.shape[1]
    turn = pick_matrix(16, OWN, [lambda row, col: row == col])
    w_own[...] = jnp.zeros((16, FW + 256), BF)
    w_own[pl.ds(0, OWN), pl.ds(0, width)] = h_in[...]
    o_own[...] = jnp.zeros((16, FW), BF)
    o_own[:, pl.ds(0, width)] = contract_last(turn, o_in[...]).astype(BF)
    w_own[:, pl.ds(FW, 256)] = o_own[:, pl.ds(0, 256)]
    for u in range(7):
        for v in range(OWN):
            w_own[pl.ds(OWN + u, 1), pl.ds(128 * v, 128)] = o_own[pl.ds(v, 1), pl.ds(256 + 128 * u, 128)]

    bar = pltpu.get_barrier_semaphore()

    def signal(device):
        pl.semaphore_signal(bar, inc=1, device_id=device, device_id_type=MESH)

    beyond = (ring_y(lax.rem(y + 2, NY)), ring_y(lax.rem(y + NY - 2, NY)))
    for device in (core, pair, far, x_up, x_dn, z_up, z_dn, last, after, *beyond):
        signal(device)
    for k in takers + holders:

        @pl.when(other(k))
        def _():
            signal(ring_y(k))

    pl.semaphore_wait(bar, 19 - 2 * mine.astype(jnp.int32))

    def half(ref, n):
        return ref.at[:, pl.ds(*SPANS[n])]

    def y_copy(n, i):
        to = wy.at[slab(lo, 16), pl.ds(*SPANS[n])]
        return remote(half(w_own, n), to, y_ss.at[n, i], y_rs.at[n, lo], ring_y(takers[i]))

    def y_sent():
        for n in range(2):
            for i in range(4):

                @pl.when(other(takers[i]))
                def _():
                    y_copy(n, i).wait_send()

    def y_wait(n):
        for l in range(NLO):

            @pl.when(other(holders[l]))
            def _():
                came = wy.at[slab(l, 16), pl.ds(*SPANS[n])]
                remote(half(w_own, n), came, y_ss.at[n, 0], y_rs.at[n, l], pair).wait_recv()

    for n in range(2):
        for i in range(4):

            @pl.when(other(takers[i]))
            def _():
                y_copy(n, i).start()

            @pl.when(takers[i] == y)
            def _():
                wy[slab(lo, 16), pl.ds(*SPANS[n])] = w_own[:, pl.ds(*SPANS[n])]

    net.sends.append(y_sent)
    net.arrivals["y", 0] = lambda: y_wait(0)
    net.arrivals["y", 1] = lambda: y_wait(1)

    @pl.loop(0, 9)
    def _(k):
        rows = lax.broadcasted_iota(jnp.int32, (128, D), 0) + k * 128
        perm[slab(k, 128), :] = jnp.where(rows == order[...], 1.0, 0.0).astype(BF)

    gain = gain_in[...].reshape(1, D)
    high = gain.astype(BF)
    middle = (gain - high.astype(F32)).astype(BF)
    low = (gain - high.astype(F32) - middle.astype(F32)).astype(BF)
    three = jnp.concatenate([high, middle, low, jnp.zeros((13, D), BF)], axis=0)

    def permute_text(cols):
        terms = jnp.dot(three, perm[:, cols], preferred_element_type=F32)
        gperm[:, cols] = jnp.sum(terms, axis=0, keepdims=True)
        tp[:, cols] = jnp.dot(text[...], perm[:, cols], preferred_element_type=F32).astype(BF)

    column_loop(permute_text)

    tx = tp[...].astype(F32)
    text_norm = jnp.sqrt(jnp.sum(tx * tx, axis=1, keepdims=True) + EPS)
    tz[pl.ds(64, 64), :] = (tx / text_norm).astype(BF)
    for d, (device, back) in enumerate(((after, last), (last, after))):
        mine_tz, there, here = tz.at[pl.ds(64, 64)], tz.at[pl.ds(128 * d, 64)], tz.at[pl.ds(128 * d, 64)]
        net.start(
            remote(mine_tz, there, tz_ss.at[d], tz_rs.at[d], device), ("tz", d),
            remote(mine_tz, here, tz_ss.at[d], tz_rs.at[d], back),
        )

    def text_slot(to, source, d):
        return 4 * d + source % NLO - (to % NLO) // 2 * 2

    def each_text(act):
        for (source, d), ways in ROUTES.items():
            for way in (0, 1):
                stops = (source, *ways[way])
                for hop in range(len(stops) - 1):
                    act(d, stops[hop], hop, way, source, stops[hop + 1])

    def tx_copy(d, at, hop, way, source, to):
        if hop == 0:
            src, sem = tz.at[pl.ds(64 * d, 64)], tx_ss.at[d, way]
        else:
            j = text_slot(at, source, d)
            src, sem = texts.at[pl.ds(64 * j, 64)], tf_ss.at[j]
        j = text_slot(to, source, d)
        return remote(src, texts.at[pl.ds(64 * j, 64)], sem, tx_rs.at[j], ring_y(jnp.int32(to)))

    def tx_came(j):
        remote(tz.at[pl.ds(64, 64)], texts.at[pl.ds(64 * j, 64)], tx_ss.at[0, 0], tx_rs.at[j], pair).wait_recv()

    passing = set()
    each_text(lambda d, at, hop, way, source, to: hop and passing.add((at, text_slot(at, source, d))))

    def tx_send(depth, column):
        def act(d, at, hop, way, source, to):
            if (hop, d) == (depth, column):

                @pl.when(y == at)
                def _():
                    if hop:
                        tx_came(text_slot(at, source, d))
                    tx_copy(d, at, hop, way, source, to).start()

        each_text(act)

    def tx_keep(d):
        for at in range(NY):
            j = text_slot(at, at, d)
            if at // NLO == at % 2 and 0 <= j <= 8:

                @pl.when(y == at)
                def _():
                    texts[pl.ds(64 * j, 64), :] = tz[pl.ds(64 * d, 64), :]

    def tx_sent():
        def act(*hop):
            @pl.when(y == hop[1])
            def _():
                tx_copy(*hop).wait_send()

        each_text(act)

    def tx_wait():
        for j in range(9):
            done = mine & (p == j % 4)
            for at in range(NY):
                if (at, j) in passing:
                    done = done | (y == at)

            @pl.when(jnp.logical_not(done))
            def _():
                tx_came(j)

    net.sends.append(tx_sent)
    net.arrivals["tx"] = tx_wait
    texts[slab(9, 64), :] = jnp.zeros((64, D), BF)

    def place(x_at, z_at, rows):
        return (x_at * NZ + z_at) * rows

    def x_of(rel):
        return lax.rem(x + rel + NX, NX)

    def z_of(rel):
        return lax.rem(z + rel + NZ, NZ)

    rings = {}

    def ring(key, buf, rows, size, pos, at, peers, ss, rs, last):
        rings.setdefault(key, []).append(
            Ring(net, buf, rows, size, pos, at, peers, lambda step, way: (ss.at[step, way], rs.at[step, way]), last)
        )

    ups, zs = (x_up, x_dn), (z_up, z_dn)
    ring(("Ax", 0), hm, MAIN, NX, x, lambda k: place(k, z, MAIN), ups, ax_ss, ax_rs, None)
    for n, rel in enumerate((0, -1, 1, 2)):
        ring(
            ("Az", rel), hm, MAIN, NZ, z, lambda k, rel=rel: place(x_of(rel), k, MAIN), zs,
            az_ss.at[n], az_rs.at[n], None,
        )
    for n, (buf, rows) in enumerate(((om, MAIN), (rest, 16))):
        ring(
            ("Bz", 0), buf, rows, NZ, z, lambda k, rows=rows: place(x, k, rows), zs,
            bz_ss.at[n], bz_rs.at[n], 0 if n else None,
        )
        for m, rel in enumerate((0, -1, 1, -2, 2, -3, 3, 4)):
            ring(
                ("Bx", rel), buf, rows, NX, x, lambda k, rel=rel, rows=rows: place(k, z_of(rel), rows), ups,
                bx_ss.at[n, m], bx_rs.at[n, m], m % 2 if n else None,
            )

    def begin(key):
        for one in rings[key]:
            one.send(1)

    net.wait(("y", 0))
    keep = pick_matrix(MAIN, 64, [lambda row, col: row == lax.shift_right_logical(col, 4) * OWN + (col & 15)])
    keep = jnp.where((lax.broadcasted_iota(jnp.int32, (MAIN, 64), 1) & 15) < OWN, keep, jnp.zeros_like(keep))
    mine_main = pl.ds(pl.multiple_of(place(x, z, MAIN), MAIN), MAIN)
    hm[mine_main, :] = jnp.dot(keep, wy[:, pl.ds(0, FW)], preferred_element_type=F32).astype(BF)
    begin(("Az", 0))
    begin(("Ax", 0))
    for v in range(OWN):
        stack[pl.ds(64 * v, 64), :] = wy[:, pl.ds(128 * v, 128)]
    for u in range(7):
        pick = pick_matrix(64, 64 * OWN, [lambda row, col: col == (row & 15) * 64 + (row & 48) + OWN + u])
        wo[:, pl.ds(256 + 128 * u, 128)] = jnp.dot(pick, stack[...], preferred_element_type=F32).astype(BF)
    net.wait(("y", 1))
    wo[:, pl.ds(0, 256)] = wy[:, pl.ds(FW, 256)]
    om[mine_main, :] = jnp.dot(keep, wo[...], preferred_element_type=F32).astype(BF)
    folded = jnp.zeros((16, 640), F32)
    for u, (lane, lanes) in enumerate(FOLDS):
        pick = pick_matrix(16, 64, [lambda row, col: ((row & 3) == u) & (col == 48 + 5 + lax.shift_right_logical(row, 2))])
        held = wy[:, pl.ds(lane, lanes)] if lane < FW else wo[:, pl.ds(lane - FW, lanes)]
        got = jnp.dot(pick, held, preferred_element_type=F32)
        if lanes < 640:
            got = jnp.concatenate([got, jnp.zeros((16, 640 - lanes), F32)], axis=1)
        folded = folded + got
    rest[pl.ds(pl.multiple_of(place(x, z, 16), 16), 16), :] = folded.astype(BF)
    for key in (("Bz", 0), ("Bx", 0)):
        begin(key)

    def im_copy(k, block):
        return remote(
            images.at[slab(2 * h + k, 64)], xin.at[slab(2 * k + block, 64)], im_ss.at[k], im_rs.at[k], pair
        )

    for k in range(2):
        net.start(im_copy(k, p), ("im", k), im_copy(k, 1 - p))
        xin[slab(2 * k + p, 64), :] = images[slab(2 * h + k, 64), :]

    def text_start(d):
        if d != 1:
            net.wait(("tz", d // 2))
        tx_send(0, d)
        tx_keep(d)

    beside = {0: lambda: text_start(1), 4: lambda: text_start(0), 5: lambda: text_start(2)}
    for n, hop in ((20, (1, 1)), (24, (1, 0)), (26, (1, 2)), (31, (2, 1)), (34, (2, 0)), (36, (2, 2))):
        beside[n] = lambda hop=hop: tx_send(*hop)

    def normed_rows():
        for k in range(2):
            net.wait(("im", k))

        def permute_images(cols):
            xp[:, cols] = jnp.dot(xin[...], perm[:, cols], preferred_element_type=F32).astype(BF)

        column_loop(permute_images)

        @pl.loop(0, 4)
        def _(r):
            xhat, _ = ln_stats(xp[slab(r, 64), :].astype(F32))
            npm[slab(r, 64), :] = (xhat * gperm[...]).astype(BF)

    for n, (route, rel, step) in enumerate(ARRIVALS):
        for one in rings[route, rel]:
            one.forward(step)
        if route == "Ax":
            for k in ((-1, 1), (2,))[step - 1]:
                begin(("Az", k))
        if route == "Bz":
            for k in (-step, step) if step < 4 else (4,):
                begin(("Bx", k))
        if n in beside:
            beside[n]()
        if n == 30:
            normed_rows()

    def unfold(u, buf, lane, lanes):
        tests = [lambda row, col: col == lax.shift_right_logical(row, 2) * 16 + (row & 3) * 4 + u]
        got = jnp.dot(pick_matrix(128, 512, tests), rest[:, pl.ds(0, lanes)], preferred_element_type=F32)
        buf[pl.ds(1024, 128), pl.ds(lane, lanes)] = got.astype(BF)

    for u, (lane, lanes) in enumerate(FOLDS):
        unfold(u, hm if lane < FW else om, lane % FW, lanes)

    def hidden(cols):
        v = jnp.dot(npm[...], hm[:, cols], preferred_element_type=F32)
        preact[:, cols] = v
        act[:, cols] = (0.5 * v * (1.0 + jnp.tanh(GELU_C * (v + GELU_A * (v * v * v))))).astype(BF)

    column_loop(hidden)

    def head_terms(cols):
        part[:, cols] = contract_last(act[...], om[cols, :])

    column_loop(head_terms)

    def swap(n, src, dst, device, comes=None):
        def copy(src, dst):
            return remote(src, dst, sw_ss.at[n], sw_rs.at[n], device)

        net.start(copy(src, dst), n, comes is not None and copy(comes, comes))

    def core_send(n, k, at, b):
        rows = pl.ds(128 * k + 64 * at, 64)
        cs[rows, :] = part[slab(2 * (1 - c) + b, 64), :].astype(BF)
        swap(n + at, cs.at[rows], cr.at[rows], core)

    def core_add(n, k, at, b):
        net.wait(n + at)
        rows = pl.ds(128 * k + 64 * at, 64)
        accb[slab(b, 64), :] = part[slab(2 * c + b, 64), :] + cr[rows, :].astype(F32)

    def pair_send(n, k, at, b):
        rows = pl.ds(128 * k + 64 * at, 64)
        es[rows, :] = accb[slab(b, 64), :].astype(BF)
        swap(n + at, es.at[rows], er.at[rows], pair)

    def sum_start(n, k, beside=lambda: None):
        for b in range(2):
            core_send(n, k, b, b)
        beside()
        for b in range(2):
            core_add(n, k, b, b)
            pair_send(n + 2, k, b, b)

    def sum_end(n, k, b):
        net.wait(n + 2 + b)
        return accb[slab(b, 64), :] + er[pl.ds(128 * k + 64 * b, 64), :].astype(F32)

    def share(n, ref, b):
        rows, comes = slab(2 * c + b, 64), slab(2 * (1 - c) + b, 64)
        swap(n + b, ref.at[rows], ref.at[rows], core, ref.at[comes])

    sum_start(0, 0)

    def gelu_slope(cols):
        v = preact[:, cols]
        th = jnp.tanh(GELU_C * (v + GELU_A * (v * v * v)))
        inner = GELU_C * (1.0 + (3.0 * GELU_A) * (v * v))
        dgel[:, cols] = 0.5 * (1.0 + th) + 0.5 * v * (1.0 - th * th) * inner

    column_loop(gelu_slope)
    for b in range(2):
        rows = slab(b, 64)
        out = xp[slab(2 * c + b, 64), :].astype(F32) + sum_end(0, 0, b)
        norm = jnp.sqrt(jnp.sum(out * out, axis=1, keepdims=True) + EPS)
        out = out / norm
        head[rows, :] = out
        inorm[rows, :] = jnp.broadcast_to(norm, (64, 128))
        unit[slab(2 * c + b, 64), :] = out.astype(BF)
        share(4, unit, b)
    net.wait("tx")
    for b in range(2):
        net.wait(4 + b)

    own_quarter = 2 * h

    def slope(dots, row, col):
        block = lax.shift_right_logical(row, 6) & 1
        scored = (col >= block * 64) & (col < 512 + block * 64)
        match = (col == 256 + block * 64 + (row & 63)) & (lax.shift_right_logical(row, 7) + own_quarter == q)
        value = jax.nn.sigmoid(SCALE_LOGIT * dots + BIAS_LOGIT) - jnp.where(match, 1.0, 0.0)
        return jnp.where(scored, SCALE_LOGIT * value, 0.0).astype(BF)

    @pl.loop(0, 5)
    def _(k):
        cols = slab(k, 128)
        row = lax.broadcasted_iota(jnp.int32, (256, 128), 0)
        col = lax.broadcasted_iota(jnp.int32, (256, 128), 1) + k * 128
        slopes[:, cols] = slope(contract_last(unit[...], texts[cols, :]), row, col)

    def to_image(cols):
        part[:, cols] = jnp.dot(slopes[...], texts[:, cols], preferred_element_type=F32)

    column_loop(to_image)

    def text_slopes():
        @pl.loop(0, 5)
        def _(k):
            rows = slab(k, 128)
            row = lax.broadcasted_iota(jnp.int32, (128, 256), 1)
            col = lax.broadcasted_iota(jnp.int32, (128, 256), 0) + k * 128
            slopes_t[rows, :] = slope(contract_last(texts[rows, :], unit[...]), row, col)

    sum_start(6, 1, text_slopes)

    def gz_part(k, d, r):
        device, buf = ((last, from_next), (after, from_last))[d]
        there = buf.at[pl.ds(64 * r, 64)]
        j = 8 * d + r - 2 * k
        return remote(tgs.at[pl.ds(64 * j, 64)], there, gz_ss.at[d, r], gz_rs.at[d, r], device)

    gz_parts = [(k, d, r) for k in range(2) for d in range(2) for r in range(NLO) if 0 <= 8 * d + r - 2 * k <= 8]

    def gz_each(pick, act):
        for k, d, r in gz_parts:
            if pick(8 * d + r - 2 * k):

                @pl.when(kk == k)
                def _():
                    act(gz_part(k, d, r))

    for k in (0, 4, 1, 3, 2):
        rows = pl.ds(128 * k, 128)

        def to_text(cols):
            tgs[rows, cols] = jnp.dot(slopes_t[rows, :], unit[:, cols], preferred_element_type=F32).astype(BF)

        column_loop(to_text)
        gz_each(lambda j: j // 2 == k, lambda copy: copy.start())
    net.sends.append(lambda: gz_each(lambda j: True, lambda copy: copy.wait_send()))

    def tg_copy(r):
        return remote(
            tgy.at[pl.ds(64 * r, 64)], tgr.at[slab(y // 2, 64)], tg_ss.at[r], tg_rs.at[y // 2], ring_y(holders[r])
        )

    def tg_send(n):
        for k in range(2):

            @pl.when(kk == k)
            def _():
                tg_row(k, (n + 2 * k) % NLO)

    def tg_row(k, r):
        for part in gz_parts:
            if part[0] == k and part[2] == r:
                gz_part(*part).wait_recv()
        rows = pl.ds(64 * r, 64)
        own = tgs[pl.ds(64 * (4 + r - 2 * k), 64), :].astype(F32)
        total = (own + from_next[rows, :].astype(F32) + from_last[rows, :].astype(F32)).astype(BF)
        tgy[rows, :] = total

        @pl.when(other(holders[r]))
        def _():
            tg_copy(r).start()

        @pl.when(holders[r] == y)
        def _():
            tgr[slab(y // 2, 64), :] = total

    def tg_sent():
        for r in range(NLO):

            @pl.when(other(holders[r]))
            def _():
                tg_copy(r).wait_send()

    def tg_wait():
        for i in range(4):

            @pl.when(other(takers[i]))
            def _():
                remote(
                    tgy.at[pl.ds(0, 64)], tgr.at[pl.ds(64 * i, 64)], tg_ss.at[0], tg_rs.at[i], pair
                ).wait_recv()

    tg_send(0)
    tg_send(1)

    for b in range(2):
        rows = slab(b, 64)
        g = sum_end(6, 1, b)
        f = head[rows, :]
        out = (g - f * jnp.sum(f * g, axis=1, keepdims=True)) / inorm[rows, 0:1]
        gout[rows, :] = out
        gob[slab(2 * c + b, 64), :] = out.astype(BF)
        share(10, gob, b)

    net.sends.append(tg_sent)
    net.arrivals["tg"] = tg_wait
    tg_send(2)
    for b in range(2):
        net.wait(10 + b)

    def hidden_back(cols):
        g = jnp.dot(gob[...], om[:, cols], preferred_element_type=F32)
        gpre[:, cols] = (g * dgel[:, cols]).astype(BF)

    column_loop(hidden_back)
    tg_send(3)

    def normed_terms(cols):
        part[:, cols] = contract_last(gpre[...], hm[cols, :])

    column_loop(normed_terms)
    core_send(12, 2, 0, 1 - p)
    core_send(12, 2, 1, p)
    core_add(12, 2, 0, 1 - p)
    pair_send(14, 2, 0, 1 - p)
    core_add(12, 2, 1, p)
    xhat, rdev = ln_stats(xp[slab(2 * c + p, 64), :].astype(F32))
    net.wait(14)
    g = (accb[slab(p, 64), :] + er[pl.ds(256, 64), :].astype(F32)) * gperm[...]
    mean_g = jnp.sum(g, axis=1, keepdims=True) * (1.0 / D)
    mean_gx = jnp.sum(g * xhat, axis=1, keepdims=True) * (1.0 / D)
    done = slab(2 * h + c, 64)
    result = (gout[slab(p, 64), :] + rdev * (g - mean_g - xhat * mean_gx)).astype(BF)

    def natural_image(cols):
        out_img[done, cols] = contract_last(result, perm[cols, :]).astype(BF)

    column_loop(natural_image)
    from_far, from_core, from_both = slab(2 * (1 - h) + c, 64), slab(2 * h + 1 - c, 64), slab(2 * (1 - h) + 1 - c, 64)
    swap(15, out_img.at[done], out_img.at[done], far, out_img.at[from_far])
    swap(16, out_img.at[done], out_img.at[done], core, out_img.at[from_core])

    net.wait("tg")
    g = tgr[pl.ds(0, 64), :].astype(F32)
    for k in range(1, 4):
        g = g + tgr[slab(k, 64), :].astype(F32)
    tx = tp[...].astype(F32)
    text_norm = jnp.sqrt(jnp.sum(tx * tx, axis=1, keepdims=True) + EPS)
    text_f = tx / text_norm
    g = (g - text_f * jnp.sum(text_f * g, axis=1, keepdims=True)) / text_norm
    high = g.astype(BF)
    both = jnp.concatenate([high, (g - high.astype(F32)).astype(BF)], axis=0)

    def natural_text(cols):
        got = contract_last(both, perm[cols, :])
        out_text[:, cols] = got[:64] + got[64:]

    column_loop(natural_text)
    net.wait(15)
    swap(17, out_img.at[from_far], out_img.at[from_far], core, out_img.at[from_both])


def kernel(*refs):
    net = Net()
    stages(net, *refs)
    net.drain()


def feature_order():
    first = (np.arange(NX * NZ) * (MAIN + REST))[:, None]
    main = (first + np.arange(MAIN)).reshape(-1)
    rest = (first + MAIN + np.arange(REST)).reshape(-1)
    return np.concatenate([main, rest]).reshape(1, D).astype(np.int32)


def shards(images, layer_norm_gain, hidden_weight, output_weight, text):

    def vm(rows, cols, kind=BF):
        return pltpu.VMEM((rows, cols), kind)

    dma = pltpu.SemaphoreType.DMA
    scratch = [
        vm(16, FW + 256), vm(16, FW), vm(64, FW + 256), vm(64, FW), vm(64 * OWN, 128), vm(D, FW), vm(D, FW), vm(512, 640),
        vm(256, D), vm(256, D), vm(D, D), vm(256, D), vm(1, D, F32),
        vm(256, FW), vm(256, FW, F32), vm(256, FW, F32), vm(256, D, F32),
        vm(384, D), vm(384, D), vm(320, D), vm(320, D),
        vm(256, D), vm(128, D, F32), vm(128, 128, F32), vm(128, D, F32), vm(256, D), vm(256, FW),
        vm(640, D), vm(192, D), vm(640, D), vm(256, D), vm(256, D), vm(256, D), vm(256, D), vm(256, 640), vm(640, 256), vm(128, D, F32), vm(64, D),
        dma((2, 4)), dma((2, 4)), dma((2,)), dma((2,)),
        dma((2, 2)), dma((2, 2)), dma((4, 4, 2)), dma((4, 4, 2)),
        dma((2, 4, 2)), dma((2, 4, 2)), dma((2, 8, 2, 2)), dma((2, 8, 2, 2)),
        dma((2,)), dma((2,)), dma((3, 2)), dma((9,)), dma((9,)), dma((2, 4)), dma((2, 4)), dma((4,)), dma((4,)), dma((18,)), dma((18,)),
    ]
    vmem = pl.BlockSpec(memory_space=pltpu.VMEM)
    images_gradient, grad_text = pl.pallas_call(
        kernel,
        out_shape=(jax.ShapeDtypeStruct((256, D), BF), jax.ShapeDtypeStruct((64, D), F32)),
        in_specs=[vmem] * 6,
        out_specs=(vmem, vmem),
        scratch_shapes=scratch,
        compiler_params=pltpu.CompilerParams(
            collective_id=0, has_side_effects=True, vmem_limit_bytes=56 * 2**20
        ),
        cost_estimate=pl.CostEstimate(flops=4 * 10**9, bytes_accessed=4 * 10**6, transcendentals=10**6),
    )(images, layer_norm_gain, hidden_weight, output_weight, text, jnp.asarray(feature_order()))
    return images_gradient.astype(F32), grad_text


def solution(mesh):
    placed = (P("dp", None), P(), P("dp", "tensor"), P("tensor", "dp"), P(("dp", "tensor"), None))
    return jax.shard_map(
        shards,
        mesh=mesh,
        in_specs=placed,
        out_specs=(P("dp", None), P(("dp", "tensor"), None)),
        check_vma=False,
    )
```

```python
import jax
import jax.numpy as jnp
import numpy as np
from jax import lax
from jax.experimental import pallas as pl
from jax.experimental.pallas import tpu as pltpu
from jax.sharding import PartitionSpec as P

SCALE_LOGIT = 10.0
BIAS_LOGIT = -3.0
EPS = 1e-06

NX, NZ, NY, NLO = 4, 8, 8, 4
D = 1152
FW = 1152
MAIN, REST = 32, 4
FOLDS = ((0, 640), (640, 512), (1152, 640), (1792, 512))
OWN = 9
SPANS = ((0, FW), (FW, 256))
ARRIVALS = (
    ("Az", 0, 1), ("Bx", 0, 1), ("Bz", 0, 1), ("Ax", 0, 1), ("Bx", 0, 2), ("Az", 0, 2), ("Bx", -1, 1), ("Bz", 0, 2),
    ("Az", -1, 1), ("Bx", 1, 1), ("Ax", 0, 2), ("Az", 1, 1), ("Bx", -1, 2), ("Az", 0, 3), ("Bx", -2, 1), ("Bz", 0, 3),
    ("Bx", 2, 1), ("Az", -1, 2), ("Bx", 1, 2), ("Bx", -2, 2), ("Az", 2, 1), ("Az", 1, 2), ("Bx", -3, 1), ("Az", 0, 4),
    ("Bz", 0, 4), ("Bx", 3, 1), ("Bx", 2, 2), ("Az", -1, 3), ("Bx", -3, 2), ("Az", 2, 2), ("Bx", 4, 1), ("Az", 1, 3),
    ("Bx", 3, 2), ("Az", -1, 4), ("Bx", 4, 2), ("Az", 2, 3), ("Az", 1, 4), ("Az", 2, 4),
)
MESH = pl.DeviceIdType.MESH
BF = jnp.bfloat16
F32 = jnp.float32
GELU_C = 0.7978845608028654
GELU_A = 0.044715


def contract_last(left, right):
    return lax.dot_general(left, right, (((1,), (1,)), ((), ())), preferred_element_type=F32)


def ident(x, z, y, c):
    return (x * (NZ * NLO) + z * NLO + lax.rem(y, NLO), (y // NLO) * 2 + c)


ROUTES = {
    (0, 0): ((4,), ()),
    (0, 1): ((), (6, 4, 2)),
    (0, 2): ((2, 4, 6), ()),
    (1, 0): ((4,), (0,)),
    (1, 1): ((2,), (0, 6, 4)),
    (1, 2): ((2,), (6,)),
    (2, 0): ((), (0, 6, 4)),
    (2, 1): ((4, 6, 0), ()),
    (2, 2): ((6,), ()),
    (3, 0): ((4,), (2, 0, 6)),
    (3, 1): ((4, 6), (2, 0)),
    (4, 0): ((5,), (1,)),
    (4, 1): ((5,), (3, 1, 7)),
    (4, 2): ((5, 7), (3, 1)),
    (5, 0): ((1,), ()),
    (5, 1): ((), (3, 1, 7)),
    (5, 2): ((7,), (3,)),
    (6, 0): ((7, 1), (5, 3)),
    (6, 1): ((7, 1, 3), (5,)),
    (6, 2): ((7,), (3,)),
    (7, 0): ((1, 3), (5,)),
    (7, 1): ((1, 3), (5,)),
}


class Net:
    def __init__(self):
        self.sends, self.arrivals = [], {}

    def start(self, copy, name, arrival=None):
        copy.start()
        self.sends.append(copy.wait_send)
        self.arrivals[name] = (arrival or copy).wait_recv

    def wait(self, name):
        self.arrivals.pop(name)()

    def drain(self):
        for name in list(self.arrivals):
            self.wait(name)
        for wait_send in self.sends:
            wait_send()


class Ring:
    def __init__(self, net, buf, rows, size, pos, at, peers, sems, last):
        self.net, self.buf, self.rows, self.size, self.pos, self.at = net, buf, rows, size, pos, at
        self.peers, self.sems, self.last = peers, sems, last
        self.steps = size // 2

    def part(self, step, way):
        if step < self.steps:
            return 0, self.rows
        if self.last is None:
            return way * (self.rows // 2), self.rows // 2
        return (0, self.rows) if way == self.last else None

    def copy(self, step, way, back):
        slot = lax.rem(self.pos + (-back if way == 0 else back) + 2 * self.size, self.size)
        off, rows = self.part(step, way)
        ref = self.buf.at[pl.ds(pl.multiple_of(self.at(slot) + off, 16), rows)]
        ssem, rsem = self.sems(step - 1, way)
        return pltpu.make_async_remote_copy(
            src_ref=ref, dst_ref=ref, send_sem=ssem, recv_sem=rsem, device_id=self.peers[way], device_id_type=MESH
        )

    def send(self, step):
        for way in (0, 1):
            if self.part(step, way):
                self.go(step, way)

    def go(self, step, way):
        self.net.start(self.copy(step, way, step - 1), (self, step, way), self.copy(step, way, step))

    def forward(self, step):
        for way in (0, 1):
            if self.part(step, way):
                self.net.wait((self, step, way))
                if step < self.steps and self.part(step + 1, way):
                    self.go(step + 1, way)


def pick_matrix(rows, cols, pairs):
    row = lax.broadcasted_iota(jnp.int32, (rows, cols), 0)
    col = lax.broadcasted_iota(jnp.int32, (rows, cols), 1)
    hit = jnp.zeros((rows, cols), F32)
    for test in pairs:
        hit = jnp.where(test(row, col), 1.0, hit)
    return hit.astype(BF)


def column_loop(body):
    @pl.loop(0, 3)
    def _(k):
        body(pl.ds(pl.multiple_of(k * 384, 128), 384))


def ln_stats(v):
    v = v - jnp.sum(v, axis=1, keepdims=True) * (1.0 / D)
    var = jnp.sum(v * v, axis=1, keepdims=True) * (1.0 / D)
    rdev = 1.0 / jnp.sqrt(var + EPS)
    return v * rdev, rdev


def stages(
    net, images, gain_in, h_in, o_in, text, order,
    out_full, out_text,
    w_own, o_own, wy, wo, stack, hm, om, rest, xin, xp, perm, npm, gperm, act, preact, dgel, part,
    cs, cr, es, er, unit, head, inorm, gout, gob, gpre, texts, tz, tgs, from_next, from_last, tgy, tgr, slopes, slopes_t, accb, tp, out_img,
    y_ss, y_rs, im_ss, im_rs, ax_ss, ax_rs, az_ss, az_rs, bz_ss, bz_rs, bx_ss, bx_rs,
    tz_ss, tz_rs, tx_ss, tf_ss, tx_rs, gz_ss, gz_rs, tg_ss, tg_rs, sw_ss, sw_rs,
):
    a = lax.axis_index("dp")
    t = lax.axis_index("tensor")
    x, z, lo = a // (NZ * NLO), lax.rem(a // NLO, NZ), lax.rem(a, NLO)
    h, c = t // 2, lax.rem(t, 2)
    y = h * NLO + lo
    p = lax.rem(lo, 2)
    q = p * 2 + c
    kk = lo // 2
    n_dp = NX * NZ * NLO
    mine = p == h

    core = ident(x, z, y, 1 - c)
    pair = ident(x, z, y + 1 - 2 * p, c)
    far = ident(x, z, lax.rem(y + NLO, NY), c)
    x_up = ident(lax.rem(x + 1, NX), z, y, c)
    x_dn = ident(lax.rem(x + NX - 1, NX), z, y, c)
    z_up = ident(x, lax.rem(z + 1, NZ), y, c)
    z_dn = ident(x, lax.rem(z + NZ - 1, NZ), y, c)

    last = (lax.rem(a - NLO + n_dp, n_dp), t)
    after = (lax.rem(a + NLO, n_dp), t)

    def ring_y(k):
        return ident(x, z, k, c)

    def when(*conditions):
        live = [k for k in conditions if not isinstance(k, bool)]
        if not all(k for k in conditions if isinstance(k, bool)):
            return lambda body: None
        if not live:
            return lambda body: body()
        both = live[0]
        for k in live[1:]:
            both = both & k
        return pl.when(both)

    takers = [h + 2 * i for i in range(4)]
    holders = [4 * p + l for l in range(NLO)]

    def other(k):
        return jnp.logical_not(k == y)

    def remote(src, dst, ss, rs, device):
        return pltpu.make_async_remote_copy(
            src_ref=src, dst_ref=dst, send_sem=ss, recv_sem=rs, device_id=device, device_id_type=MESH
        )

    def slab(k, rows):
        return pl.ds(k * rows if isinstance(k, int) else pl.multiple_of(k * rows, rows), rows)

    from_next[...] = jnp.zeros((256, D), BF)
    from_last[...] = jnp.zeros((256, D), BF)
    width = h_in.shape[1]
    turn = pick_matrix(16, OWN, [lambda row, col: row == col])
    w_own[...] = jnp.zeros((16, FW + 256), BF)
    w_own[pl.ds(0, OWN), pl.ds(0, width)] = h_in[...]
    o_own[...] = jnp.zeros((16, FW), BF)
    o_own[:, pl.ds(0, width)] = contract_last(turn, o_in[...]).astype(BF)
    w_own[:, pl.ds(FW, 256)] = o_own[:, pl.ds(0, 256)]
    for u in range(7):
        for v in range(OWN):
            w_own[pl.ds(OWN + u, 1), pl.ds(128 * v, 128)] = o_own[pl.ds(v, 1), pl.ds(256 + 128 * u, 128)]

    bar = pltpu.get_barrier_semaphore()

    def signal(device):
        pl.semaphore_signal(bar, inc=1, device_id=device, device_id_type=MESH)

    beyond = (ring_y(lax.rem(y + 2, NY)), ring_y(lax.rem(y + NY - 2, NY)))
    for device in (core, pair, far, x_up, x_dn, z_up, z_dn, last, after, *beyond):
        signal(device)
    for k in takers + holders:

        @pl.when(other(k))
        def _():
            signal(ring_y(k))

    pl.semaphore_wait(bar, 19 - 2 * mine.astype(jnp.int32))

    def half(ref, n):
        return ref.at[:, pl.ds(*SPANS[n])]

    def y_copy(n, i):
        to = wy.at[slab(lo, 16), pl.ds(*SPANS[n])]
        return remote(half(w_own, n), to, y_ss.at[n, i], y_rs.at[n, lo], ring_y(takers[i]))

    def y_sent():
        for n in range(2):
            for i in range(4):

                @pl.when(other(takers[i]))
                def _():
                    y_copy(n, i).wait_send()

    def y_wait(n):
        for l in range(NLO):

            @pl.when(other(holders[l]))
            def _():
                came = wy.at[slab(l, 16), pl.ds(*SPANS[n])]
                remote(half(w_own, n), came, y_ss.at[n, 0], y_rs.at[n, l], pair).wait_recv()

    for n in range(2):
        for i in range(4):

            @pl.when(other(takers[i]))
            def _():
                y_copy(n, i).start()

            @pl.when(takers[i] == y)
            def _():
                wy[slab(lo, 16), pl.ds(*SPANS[n])] = w_own[:, pl.ds(*SPANS[n])]

    net.sends.append(y_sent)
    net.arrivals["y", 0] = lambda: y_wait(0)
    net.arrivals["y", 1] = lambda: y_wait(1)

    @pl.loop(0, 9)
    def _(k):
        rows = lax.broadcasted_iota(jnp.int32, (128, D), 0) + k * 128
        perm[slab(k, 128), :] = jnp.where(rows == order[...], 1.0, 0.0).astype(BF)

    gain = gain_in[...].reshape(1, D)
    high = gain.astype(BF)
    middle = (gain - high.astype(F32)).astype(BF)
    low = (gain - high.astype(F32) - middle.astype(F32)).astype(BF)
    three = jnp.concatenate([high, middle, low, jnp.zeros((13, D), BF)], axis=0)

    def permute_text(cols):
        terms = jnp.dot(three, perm[:, cols], preferred_element_type=F32)
        gperm[:, cols] = jnp.sum(terms, axis=0, keepdims=True)
        tp[:, cols] = jnp.dot(text[...], perm[:, cols], preferred_element_type=F32).astype(BF)

    column_loop(permute_text)

    tx = tp[...].astype(F32)
    text_norm = jnp.sqrt(jnp.sum(tx * tx, axis=1, keepdims=True) + EPS)
    tz[pl.ds(64, 64), :] = (tx / text_norm).astype(BF)
    for d, (device, back) in enumerate(((after, last), (last, after))):
        mine_tz, there, here = tz.at[pl.ds(64, 64)], tz.at[pl.ds(128 * d, 64)], tz.at[pl.ds(128 * d, 64)]
        net.start(
            remote(mine_tz, there, tz_ss.at[d], tz_rs.at[d], device), ("tz", d),
            remote(mine_tz, here, tz_ss.at[d], tz_rs.at[d], back),
        )

    def text_slot(to, source, d):
        return 4 * d + source % NLO - (to % NLO) // 2 * 2

    def each_text(act):
        for (source, d), ways in ROUTES.items():
            for way in (0, 1):
                stops = (source, *ways[way])
                for hop in range(len(stops) - 1):
                    act(d, stops[hop], hop, way, source, stops[hop + 1])

    def tx_copy(d, at, hop, way, source, to):
        if hop == 0:
            src, sem = tz.at[pl.ds(64 * d, 64)], tx_ss.at[d, way]
        else:
            j = text_slot(at, source, d)
            src, sem = texts.at[pl.ds(64 * j, 64)], tf_ss.at[j]
        j = text_slot(to, source, d)
        return remote(src, texts.at[pl.ds(64 * j, 64)], sem, tx_rs.at[j], ring_y(jnp.int32(to)))

    def tx_came(j):
        remote(tz.at[pl.ds(64, 64)], texts.at[pl.ds(64 * j, 64)], tx_ss.at[0, 0], tx_rs.at[j], pair).wait_recv()

    passing = set()
    each_text(lambda d, at, hop, way, source, to: hop and passing.add((at, text_slot(at, source, d))))

    def tx_send(depth, column):
        def act(d, at, hop, way, source, to):
            if (hop, d) == (depth, column):

                @pl.when(y == at)
                def _():
                    if hop:
                        tx_came(text_slot(at, source, d))
                    tx_copy(d, at, hop, way, source, to).start()

        each_text(act)

    def tx_keep(d):
        for at in range(NY):
            j = text_slot(at, at, d)
            if at // NLO == at % 2 and 0 <= j <= 8:

                @pl.when(y == at)
                def _():
                    texts[pl.ds(64 * j, 64), :] = tz[pl.ds(64 * d, 64), :]

    def tx_sent():
        def act(*hop):
            @pl.when(y == hop[1])
            def _():
                tx_copy(*hop).wait_send()

        each_text(act)

    def tx_wait():
        for j in range(9):
            done = mine & (p == j % 4)
            for at in range(NY):
                if (at, j) in passing:
                    done = done | (y == at)

            @pl.when(jnp.logical_not(done))
            def _():
                tx_came(j)

    net.sends.append(tx_sent)
    net.arrivals["tx"] = tx_wait
    texts[slab(9, 64), :] = jnp.zeros((64, D), BF)

    def place(x_at, z_at, rows):
        return (x_at * NZ + z_at) * rows

    def x_of(rel):
        return lax.rem(x + rel + NX, NX)

    def z_of(rel):
        return lax.rem(z + rel + NZ, NZ)

    rings = {}

    def ring(key, buf, rows, size, pos, at, peers, ss, rs, last):
        rings.setdefault(key, []).append(
            Ring(net, buf, rows, size, pos, at, peers, lambda step, way: (ss.at[step, way], rs.at[step, way]), last)
        )

    ups, zs = (x_up, x_dn), (z_up, z_dn)
    ring(("Ax", 0), hm, MAIN, NX, x, lambda k: place(k, z, MAIN), ups, ax_ss, ax_rs, None)
    for n, rel in enumerate((0, -1, 1, 2)):
        ring(
            ("Az", rel), hm, MAIN, NZ, z, lambda k, rel=rel: place(x_of(rel), k, MAIN), zs,
            az_ss.at[n], az_rs.at[n], None,
        )
    for n, (buf, rows) in enumerate(((om, MAIN), (rest, 16))):
        ring(
            ("Bz", 0), buf, rows, NZ, z, lambda k, rows=rows: place(x, k, rows), zs,
            bz_ss.at[n], bz_rs.at[n], 0 if n else None,
        )
        for m, rel in enumerate((0, -1, 1, -2, 2, -3, 3, 4)):
            ring(
                ("Bx", rel), buf, rows, NX, x, lambda k, rel=rel, rows=rows: place(k, z_of(rel), rows), ups,
                bx_ss.at[n, m], bx_rs.at[n, m], m % 2 if n else None,
            )

    def begin(key):
        for one in rings[key]:
            one.send(1)

    net.wait(("y", 0))
    keep = pick_matrix(MAIN, 64, [lambda row, col: row == lax.shift_right_logical(col, 4) * OWN + (col & 15)])
    keep = jnp.where((lax.broadcasted_iota(jnp.int32, (MAIN, 64), 1) & 15) < OWN, keep, jnp.zeros_like(keep))
    mine_main = pl.ds(pl.multiple_of(place(x, z, MAIN), MAIN), MAIN)
    hm[mine_main, :] = jnp.dot(keep, wy[:, pl.ds(0, FW)], preferred_element_type=F32).astype(BF)
    begin(("Az", 0))
    begin(("Ax", 0))
    for v in range(OWN):
        stack[pl.ds(64 * v, 64), :] = wy[:, pl.ds(128 * v, 128)]
    for u in range(7):
        pick = pick_matrix(64, 64 * OWN, [lambda row, col: col == (row & 15) * 64 + (row & 48) + OWN + u])
        wo[:, pl.ds(256 + 128 * u, 128)] = jnp.dot(pick, stack[...], preferred_element_type=F32).astype(BF)
    net.wait(("y", 1))
    wo[:, pl.ds(0, 256)] = wy[:, pl.ds(FW, 256)]
    om[mine_main, :] = jnp.dot(keep, wo[...], preferred_element_type=F32).astype(BF)
    folded = jnp.zeros((16, 640), F32)
    for u, (lane, lanes) in enumerate(FOLDS):
        pick = pick_matrix(16, 64, [lambda row, col: ((row & 3) == u) & (col == 48 + 5 + lax.shift_right_logical(row, 2))])
        held = wy[:, pl.ds(lane, lanes)] if lane < FW else wo[:, pl.ds(lane - FW, lanes)]
        got = jnp.dot(pick, held, preferred_element_type=F32)
        if lanes < 640:
            got = jnp.concatenate([got, jnp.zeros((16, 640 - lanes), F32)], axis=1)
        folded = folded + got
    rest[pl.ds(pl.multiple_of(place(x, z, 16), 16), 16), :] = folded.astype(BF)
    for key in (("Bz", 0), ("Bx", 0)):
        begin(key)

    def im_copy(k, block):
        return remote(
            images.at[slab(2 * h + k, 64)], xin.at[slab(2 * k + block, 64)], im_ss.at[k], im_rs.at[k], pair
        )

    for k in range(2):
        net.start(im_copy(k, p), ("im", k), im_copy(k, 1 - p))
        xin[slab(2 * k + p, 64), :] = images[slab(2 * h + k, 64), :]

    def text_start(d):
        if d != 1:
            net.wait(("tz", d // 2))
        tx_send(0, d)
        tx_keep(d)

    beside = {0: lambda: text_start(1), 4: lambda: text_start(0), 5: lambda: text_start(2)}
    for n, hop in ((24, (1, 1)), (28, (1, 0)), (30, (1, 2)), (35, (2, 1)), (36, (2, 0)), (37, (2, 2))):
        beside[n] = lambda hop=hop: tx_send(*hop)

    def normed_rows():
        for k in range(2):
            net.wait(("im", k))

        def permute_images(cols):
            xp[:, cols] = jnp.dot(xin[...], perm[:, cols], preferred_element_type=F32).astype(BF)

        column_loop(permute_images)

        @pl.loop(0, 4)
        def _(r):
            xhat, _ = ln_stats(xp[slab(r, 64), :].astype(F32))
            npm[slab(r, 64), :] = (xhat * gperm[...]).astype(BF)

    for n, (route, rel, step) in enumerate(ARRIVALS):
        for one in rings[route, rel]:
            one.forward(step)
        if route == "Ax":
            for k in ((-1, 1), (2,))[step - 1]:
                begin(("Az", k))
        if route == "Bz":
            for k in (-step, step) if step < 4 else (4,):
                begin(("Bx", k))
        if n in beside:
            beside[n]()
        if n == 30:
            normed_rows()

    def unfold(u, buf, lane, lanes):
        tests = [lambda row, col: col == lax.shift_right_logical(row, 2) * 16 + (row & 3) * 4 + u]
        got = jnp.dot(pick_matrix(128, 512, tests), rest[:, pl.ds(0, lanes)], preferred_element_type=F32)
        buf[pl.ds(1024, 128), pl.ds(lane, lanes)] = got.astype(BF)

    for u, (lane, lanes) in enumerate(FOLDS):
        unfold(u, hm if lane < FW else om, lane % FW, lanes)

    def hidden(cols):
        v = jnp.dot(npm[...], hm[:, cols], preferred_element_type=F32)
        preact[:, cols] = v
        act[:, cols] = (0.5 * v * (1.0 + jnp.tanh(GELU_C * (v + GELU_A * (v * v * v))))).astype(BF)

    column_loop(hidden)

    def head_terms(cols):
        part[:, cols] = contract_last(act[...], om[cols, :])

    column_loop(head_terms)

    def swap(n, src, dst, device, comes=None):
        def copy(src, dst):
            return remote(src, dst, sw_ss.at[n], sw_rs.at[n], device)

        net.start(copy(src, dst), n, comes is not None and copy(comes, comes))

    def core_send(n, k, at, b):
        rows = pl.ds(128 * k + 64 * at, 64)
        cs[rows, :] = part[slab(2 * (1 - c) + b, 64), :].astype(BF)
        swap(n + at, cs.at[rows], cr.at[rows], core)

    def core_add(n, k, at, b):
        net.wait(n + at)
        rows = pl.ds(128 * k + 64 * at, 64)
        accb[slab(b, 64), :] = part[slab(2 * c + b, 64), :] + cr[rows, :].astype(F32)

    def pair_send(n, k, at, b):
        rows = pl.ds(128 * k + 64 * at, 64)
        es[rows, :] = accb[slab(b, 64), :].astype(BF)
        swap(n + at, es.at[rows], er.at[rows], pair)

    def sum_start(n, k, beside=lambda: None):
        for b in range(2):
            core_send(n, k, b, b)
        beside()
        for b in range(2):
            core_add(n, k, b, b)
            pair_send(n + 2, k, b, b)

    def sum_end(n, k, b):
        net.wait(n + 2 + b)
        return accb[slab(b, 64), :] + er[pl.ds(128 * k + 64 * b, 64), :].astype(F32)

    def share(n, ref, b):
        rows, comes = slab(2 * c + b, 64), slab(2 * (1 - c) + b, 64)
        swap(n + b, ref.at[rows], ref.at[rows], core, ref.at[comes])

    sum_start(0, 0)

    def gelu_slope(cols):
        v = preact[:, cols]
        th = jnp.tanh(GELU_C * (v + GELU_A * (v * v * v)))
        inner = GELU_C * (1.0 + (3.0 * GELU_A) * (v * v))
        dgel[:, cols] = 0.5 * (1.0 + th) + 0.5 * v * (1.0 - th * th) * inner

    column_loop(gelu_slope)
    for b in range(2):
        rows = slab(b, 64)
        out = xp[slab(2 * c + b, 64), :].astype(F32) + sum_end(0, 0, b)
        norm = jnp.sqrt(jnp.sum(out * out, axis=1, keepdims=True) + EPS)
        out = out / norm
        head[rows, :] = out
        inorm[rows, :] = jnp.broadcast_to(norm, (64, 128))
        unit[slab(2 * c + b, 64), :] = out.astype(BF)
        share(4, unit, b)
    net.wait("tx")
    for b in range(2):
        net.wait(4 + b)

    own_quarter = 2 * h

    def slope(dots, row, col):
        block = lax.shift_right_logical(row, 6) & 1
        scored = (col >= block * 64) & (col < 512 + block * 64)
        match = (col == 256 + block * 64 + (row & 63)) & (lax.shift_right_logical(row, 7) + own_quarter == q)
        value = jax.nn.sigmoid(SCALE_LOGIT * dots + BIAS_LOGIT) - jnp.where(match, 1.0, 0.0)
        return jnp.where(scored, SCALE_LOGIT * value, 0.0).astype(BF)

    @pl.loop(0, 5)
    def _(k):
        cols = slab(k, 128)
        row = lax.broadcasted_iota(jnp.int32, (256, 128), 0)
        col = lax.broadcasted_iota(jnp.int32, (256, 128), 1) + k * 128
        slopes[:, cols] = slope(contract_last(unit[...], texts[cols, :]), row, col)

    def to_image(cols):
        part[:, cols] = jnp.dot(slopes[...], texts[:, cols], preferred_element_type=F32)

    column_loop(to_image)

    def text_slopes():
        @pl.loop(0, 5)
        def _(k):
            rows = slab(k, 128)
            row = lax.broadcasted_iota(jnp.int32, (128, 256), 1)
            col = lax.broadcasted_iota(jnp.int32, (128, 256), 0) + k * 128
            slopes_t[rows, :] = slope(contract_last(texts[rows, :], unit[...]), row, col)

    sum_start(6, 1, text_slopes)

    def gz_part(k, d, r):
        device, buf = ((last, from_next), (after, from_last))[d]
        there = buf.at[pl.ds(64 * r, 64)]
        j = 8 * d + r - 2 * k
        return remote(tgs.at[pl.ds(64 * j, 64)], there, gz_ss.at[d, r], gz_rs.at[d, r], device)

    gz_parts = [(k, d, r) for k in range(2) for d in range(2) for r in range(NLO) if 0 <= 8 * d + r - 2 * k <= 8]

    def gz_each(pick, act):
        for k, d, r in gz_parts:
            if pick(8 * d + r - 2 * k):

                @pl.when(kk == k)
                def _():
                    act(gz_part(k, d, r))

    for k in (0, 4, 1, 3, 2):
        rows = pl.ds(128 * k, 128)

        def to_text(cols):
            tgs[rows, cols] = jnp.dot(slopes_t[rows, :], unit[:, cols], preferred_element_type=F32).astype(BF)

        column_loop(to_text)
        gz_each(lambda j: j // 2 == k, lambda copy: copy.start())
    net.sends.append(lambda: gz_each(lambda j: True, lambda copy: copy.wait_send()))

    def tg_copy(r):
        return remote(
            tgy.at[pl.ds(64 * r, 64)], tgr.at[slab(y // 2, 64)], tg_ss.at[r], tg_rs.at[y // 2], ring_y(holders[r])
        )

    def tg_send(n):
        for k in range(2):

            @pl.when(kk == k)
            def _():
                tg_row(k, (n + 2 * k) % NLO)

    def tg_row(k, r):
        for part in gz_parts:
            if part[0] == k and part[2] == r:
                gz_part(*part).wait_recv()
        rows = pl.ds(64 * r, 64)
        own = tgs[pl.ds(64 * (4 + r - 2 * k), 64), :].astype(F32)
        total = (own + from_next[rows, :].astype(F32) + from_last[rows, :].astype(F32)).astype(BF)
        tgy[rows, :] = total

        @pl.when(other(holders[r]))
        def _():
            tg_copy(r).start()

        @pl.when(holders[r] == y)
        def _():
            tgr[slab(y // 2, 64), :] = total

    def tg_sent():
        for r in range(NLO):

            @pl.when(other(holders[r]))
            def _():
                tg_copy(r).wait_send()

    def tg_wait():
        for i in range(4):

            @pl.when(other(takers[i]))
            def _():
                remote(
                    tgy.at[pl.ds(0, 64)], tgr.at[pl.ds(64 * i, 64)], tg_ss.at[0], tg_rs.at[i], pair
                ).wait_recv()

    tg_send(0)
    tg_send(1)

    for b in range(2):
        rows = slab(b, 64)
        g = sum_end(6, 1, b)
        f = head[rows, :]
        out = (g - f * jnp.sum(f * g, axis=1, keepdims=True)) / inorm[rows, 0:1]
        gout[rows, :] = out
        gob[slab(2 * c + b, 64), :] = out.astype(BF)
        share(10, gob, b)

    net.sends.append(tg_sent)
    net.arrivals["tg"] = tg_wait
    tg_send(2)
    for b in range(2):
        net.wait(10 + b)

    def hidden_back(cols):
        g = jnp.dot(gob[...], om[:, cols], preferred_element_type=F32)
        gpre[:, cols] = (g * dgel[:, cols]).astype(BF)

    column_loop(hidden_back)
    tg_send(3)

    def normed_terms(cols):
        part[:, cols] = contract_last(gpre[...], hm[cols, :])

    column_loop(normed_terms)
    core_send(12, 2, 0, 1 - p)
    core_send(12, 2, 1, p)
    core_add(12, 2, 0, 1 - p)
    pair_send(14, 2, 0, 1 - p)
    core_add(12, 2, 1, p)
    xhat, rdev = ln_stats(xp[slab(2 * c + p, 64), :].astype(F32))
    net.wait(14)
    g = (accb[slab(p, 64), :] + er[pl.ds(256, 64), :].astype(F32)) * gperm[...]
    mean_g = jnp.sum(g, axis=1, keepdims=True) * (1.0 / D)
    mean_gx = jnp.sum(g * xhat, axis=1, keepdims=True) * (1.0 / D)
    done = slab(2 * h + c, 64)
    result = (gout[slab(p, 64), :] + rdev * (g - mean_g - xhat * mean_gx)).astype(BF)

    def natural_image(cols):
        out_img[done, cols] = contract_last(result, perm[cols, :]).astype(BF)

    column_loop(natural_image)
    from_far, from_core, from_both = slab(2 * (1 - h) + c, 64), slab(2 * h + 1 - c, 64), slab(2 * (1 - h) + 1 - c, 64)
    swap(15, out_img.at[done], out_img.at[done], far, out_img.at[from_far])
    swap(16, out_img.at[done], out_img.at[done], core, out_img.at[from_core])

    net.wait("tg")
    g = tgr[pl.ds(0, 64), :].astype(F32)
    for k in range(1, 4):
        g = g + tgr[slab(k, 64), :].astype(F32)
    tx = tp[...].astype(F32)
    text_norm = jnp.sqrt(jnp.sum(tx * tx, axis=1, keepdims=True) + EPS)
    text_f = tx / text_norm
    g = (g - text_f * jnp.sum(text_f * g, axis=1, keepdims=True)) / text_norm
    high = g.astype(BF)
    both = jnp.concatenate([high, (g - high.astype(F32)).astype(BF)], axis=0)

    def natural_text(cols):
        got = contract_last(both, perm[cols, :])
        out_text[:, cols] = got[:64] + got[64:]

    column_loop(natural_text)
    net.wait(15)
    swap(17, out_img.at[from_far], out_img.at[from_far], core, out_img.at[from_both])


def kernel(*refs):
    net = Net()
    stages(net, *refs)
    net.drain()
    refs[6][...] = refs[46][...].astype(F32)


def feature_order():
    first = (np.arange(NX * NZ) * (MAIN + REST))[:, None]
    main = (first + np.arange(MAIN)).reshape(-1)
    rest = (first + MAIN + np.arange(REST)).reshape(-1)
    return np.concatenate([main, rest]).reshape(1, D).astype(np.int32)


def shards(images, layer_norm_gain, hidden_weight, output_weight, text):

    def vm(rows, cols, kind=BF):
        return pltpu.VMEM((rows, cols), kind)

    dma = pltpu.SemaphoreType.DMA
    scratch = [
        vm(16, FW + 256), vm(16, FW), vm(64, FW + 256), vm(64, FW), vm(64 * OWN, 128), vm(D, FW), vm(D, FW), vm(512, 640),
        vm(256, D), vm(256, D), vm(D, D), vm(256, D), vm(1, D, F32),
        vm(256, FW), vm(256, FW, F32), vm(256, FW, F32), vm(256, D, F32),
        vm(384, D), vm(384, D), vm(320, D), vm(320, D),
        vm(256, D), vm(128, D, F32), vm(128, 128, F32), vm(128, D, F32), vm(256, D), vm(256, FW),
        vm(640, D), vm(192, D), vm(640, D), vm(256, D), vm(256, D), vm(256, D), vm(256, D), vm(256, 640), vm(640, 256), vm(128, D, F32), vm(64, D), vm(256, D),
        dma((2, 4)), dma((2, 4)), dma((2,)), dma((2,)),
        dma((2, 2)), dma((2, 2)), dma((4, 4, 2)), dma((4, 4, 2)),
        dma((2, 4, 2)), dma((2, 4, 2)), dma((2, 8, 2, 2)), dma((2, 8, 2, 2)),
        dma((2,)), dma((2,)), dma((3, 2)), dma((9,)), dma((9,)), dma((2, 4)), dma((2, 4)), dma((4,)), dma((4,)), dma((18,)), dma((18,)),
    ]
    vmem = pl.BlockSpec(memory_space=pltpu.VMEM)
    return pl.pallas_call(
        kernel,
        out_shape=(jax.ShapeDtypeStruct((256, D), F32), jax.ShapeDtypeStruct((64, D), F32)),
        in_specs=[vmem] * 6,
        out_specs=(vmem, vmem),
        scratch_shapes=scratch,
        compiler_params=pltpu.CompilerParams(
            collective_id=0, has_side_effects=True, vmem_limit_bytes=56 * 2**20
        ),
        cost_estimate=pl.CostEstimate(flops=4 * 10**9, bytes_accessed=4 * 10**6, transcendentals=10**6),
    )(images, layer_norm_gain, hidden_weight, output_weight, text, jnp.asarray(feature_order()))


def solution(mesh):
    placed = (P("dp", None), P(), P("dp", "tensor"), P("tensor", "dp"), P(("dp", "tensor"), None))
    return jax.shard_map(
        shards,
        mesh=mesh,
        in_specs=placed,
        out_specs=(P("dp", None), P(("dp", "tensor"), None)),
        check_vma=False,
    )
```
